32 devices in a mesh: section: 2 (over core), shard: 4 (over y, x), replica: 4 (over z).
Axes of the slice: x: 2, y: 2, z: 4, core: 2. Of those that a mesh axis runs over, the one named last changes fastest.
Arguments:
- boundary: bfloat16 [2, 4, 48, 14, 14, 512], P('section', None, ('shard', 'replica')), may hold values from -6 to 6
- norm_gains: bfloat16 [2, 2, 512], P('section', None, 'shard'), may hold values from 0.5 to 1.5
- biases: bfloat16 [2, 6, 512], P('section', None, 'shard'), may hold values from -3 to 3
- up_bias: bfloat16 [2, 2048], P('section', 'shard'), may hold values from -3 to 3
- offset_table: bfloat16 [2, 169, 16], P('section', None, 'shard'), may hold values from -4 to 4
- attention_in: bfloat16 [2, 512, 1536], P('section', 'shard'), may hold values from -0.25 to 0.25
- attention_out: bfloat16 [2, 512, 512], P('section', 'shard'), may hold values from -1 to 1
- up_weight: bfloat16 [2, 512, 2048], P('section', 'shard'), may hold values from -0.25 to 0.25
- down_weight: bfloat16 [2, 2048, 512], P('section', 'shard'), may hold values from -0.125 to 0.125
- offset_index: int32 [49, 49], replicated, may hold values from 0 to 168
- regions: int32 [14, 14], replicated, may hold values from 0 to 3
- micro_counts: int32 [4], replicated, may hold values from 1 to 3, as said below
Outputs:
- results: bfloat16 [2, 4, 48, 14, 14, 512], P('section', None, ('shard', 'replica'))
- grad_norm_gains: float32 [2, 2, 512], P('section', None, 'shard')
- grad_biases: float32 [2, 6, 512], P('section', None, 'shard')
- grad_up_bias: float32 [2, 2048], P('section', 'shard')
- grad_offset_table: float32 [2, 169, 16], P('section', None, 'shard')
- grad_attention_in: float32 [2, 512, 1536], P('section', 'shard')
- grad_attention_out: float32 [2, 512, 512], P('section', 'shard')
- grad_up_weight: float32 [2, 512, 2048], P('section', 'shard')
- grad_down_weight: float32 [2, 2048, 512], P('section', 'shard')
The draws below stay inside these ranges and needn't reach their ends.
Inputs may be any that keep to these rules, and one draw needn't show every extreme that they name: `micro_counts`: in every draw one micro-batch has all 3 slots filled.
All inputs are finite; a program needn't handle non-finite values.
Results may differ from the reference program's by a relative error of at most 0.02.
Values may be sent and summed in bfloat16 or wider, within the bound.
No kernel may reach another device: no remote copies, remote signals or barrier semaphores. Data moves between devices by JAX's collectives and lax.ppermute only.
A program may use at most 384 MiB of HBM per device.

```python
from functools import partial
import jax
import jax.numpy as jnp
from jax import lax

D = 512
HEADS = 16
FF = 2048
WIN = 7
SIDE = 14
SHIFT = 3
REL = 169
WINS = 4
MB = 4
IMG_MB = 3
IMAGES = 48
N_SHARD = 4
N_REPLICA = 4


def draw_micro_counts(key, part):
    key = jax.random.fold_in(key, 11)
    first_key, second_key = jax.random.split(key)
    counts = jax.random.randint(first_key, (MB,), 1, IMG_MB + 1)
    chosen = jax.random.randint(second_key, (), 0, MB)
    positions = jnp.arange(MB)
    counts = jnp.where(positions == chosen, IMG_MB, counts)
    return counts.astype(jnp.int32)


def plant(drawn, own_key, least, high):
    place = [jax.random.randint(jax.random.fold_in(own_key, axis), (), 0, length) for axis, length in enumerate(drawn.shape)]
    longest = drawn.shape.index(max(drawn.shape))
    neighbour = place[:longest] + [(place[longest] + 1) % drawn.shape[longest]] + place[longest + 1:]
    return drawn.at[tuple(place)].set(least).at[tuple(neighbour)].set(high)


def block_levels(stream_key, dims, shards, least, high):
    factor_of = 1.0
    for axis_at, shards_of in shards:
        heights = jax.random.uniform(jax.random.fold_in(jax.random.fold_in(stream_key, 6), axis_at), (shards_of,), jnp.float32, least / len(shards), high / len(shards))
        factor_of = factor_of * jnp.repeat(jnp.exp(heights), dims[axis_at] // shards_of).reshape((-1,) + (1,) * (len(dims) - 1 - axis_at))
    return factor_of


def gaussian(rng, shape, scale, most, cuts=(), held_as=jnp.bfloat16):
    array = scale * jax.random.normal(rng, shape, jnp.float32)
    if cuts:
        array = array * block_levels(rng, shape, cuts, -0.22, 0.18)
    return jnp.clip(array, -most, most).astype(held_as)


def setup_inputs(seed: int = 0) -> dict:
    arg_keys = jax.random.split(jax.random.key(seed), 13)
    return {
        "boundary": gaussian(arg_keys[0], (2, MB, IMAGES, SIDE, SIDE, D), 1.0, 6.0, ((0, 2), (2, 16))),
        "norm_gains": jnp.clip(1.0 + 0.1 * jax.random.normal(arg_keys[1], (2, 2, D), jnp.float32), 0.5, 1.5).astype(jnp.bfloat16),
        "biases": gaussian(arg_keys[2], (2, 6, D), 0.5, 3.0, ((0, 2), (2, 4))),
        "up_bias": gaussian(arg_keys[3], (2, FF), 0.5, 3.0, ((0, 2), (1, 4))),
        "offset_table": gaussian(arg_keys[4], (2, REL, HEADS), 1.0, 4.0, ((0, 2), (2, 4))),
        "attention_in": gaussian(arg_keys[5], (2, D, 3 * D), D ** -0.5, 0.25, ((0, 2), (1, 4))),
        "attention_out": gaussian(arg_keys[6], (2, D, D), (D // 16) ** -0.5, 1.0, ((0, 2), (1, 4))),
        "up_weight": gaussian(arg_keys[7], (2, D, FF), D ** -0.5, 0.25, ((0, 2), (1, 4))),
        "down_weight": gaussian(arg_keys[8], (2, FF, D), FF ** -0.5, 0.125, ((0, 2), (1, 4))),
        "offset_index": plant(jax.random.randint(arg_keys[9], (WIN * WIN, WIN * WIN), 0, REL), jax.random.fold_in(arg_keys[9], 1), 0, REL - 1).astype(jnp.int32),
        "regions": plant(jax.random.randint(arg_keys[10], (SIDE, SIDE), 0, 4), jax.random.fold_in(arg_keys[10], 1), 0, 3).astype(jnp.int32),
        "micro_counts": draw_micro_counts(jax.random.fold_in(arg_keys[12], 71), 0),
    }


@jax.custom_vjp
def low(v):
    return lax.optimization_barrier(v.astype(jnp.bfloat16)).astype(jnp.float32)

@jax.custom_vjp
def low_back(v):
    return v

def low_keep(v):
    return (low(v), None)

def low_pass(kept, grad):
    return (grad,)

def back_keep(v):
    return (v, None)

def back_low(kept, grad):
    return (low(grad),)
low.defvjp(low_keep, low_pass)
low_back.defvjp(back_keep, back_low)

def norm_rows(field, gain, offset):
    average = lax.optimization_barrier(jnp.mean(field, -1, keepdims=True))
    centered = field - average
    spread = lax.optimization_barrier(jnp.mean(centered * centered, -1, keepdims=True))
    return centered * lax.rsqrt(spread + 1e-05) * gain + offset

def split_windows(field):
    images = field.shape[0]
    channels = field.shape[-1]
    per_side = SIDE // WIN
    field = field.reshape(images, per_side, WIN, per_side, WIN, channels).transpose(0, 1, 3, 2, 4, 5)
    return field.reshape(images * per_side * per_side, WIN * WIN, channels)

def merge_windows(field, images):
    channels = field.shape[-1]
    per_side = SIDE // WIN
    field = field.reshape(images, per_side, per_side, WIN, WIN, channels).transpose(0, 1, 3, 2, 4, 5)
    return field.reshape(images, SIDE, SIDE, channels)

def swin_layer(field, weights, shifted, offset_index, region_bias):
    norm_gains, biases, up_bias, offset_table, attention_in, attention_out, up_weight, down_weight = weights
    highest = lax.Precision.HIGHEST
    images = field.shape[0]
    channels = field.shape[-1]
    length = WIN * WIN
    head_size = channels // HEADS
    normed = low(norm_rows(field, norm_gains[0], biases[0]))
    if shifted:
        normed = jnp.roll(normed, (-SHIFT, -SHIFT), (1, 2))
    window_rows = split_windows(normed)
    windows = window_rows.shape[0]
    in_bias = jnp.concatenate([biases[1], jnp.zeros_like(biases[1]), biases[2]])
    projected = jnp.dot(window_rows, attention_in, precision=highest) + in_bias
    head_parts = low(low_back(projected)).reshape(windows, length, 3, HEADS, head_size)
    offsets = offset_table[offset_index].transpose(2, 0, 1)
    bias_full = offsets[None] + region_bias[:, None]
    scores = jnp.einsum('wihd,wjhd->whij', head_parts[:, :, 0], head_parts[:, :, 1], precision=highest) * head_size ** (-0.5)
    scores = scores.reshape(images, WINS, HEADS, length, length) + bias_full[None]
    scores = low_back(scores.reshape(windows, HEADS, length, length))
    probability = low(jax.nn.softmax(scores, axis=-1))
    attended = jnp.einsum('whij,wjhd->wihd', probability, head_parts[:, :, 2], precision=highest)
    attended = low(low_back(attended.reshape(windows, length, channels)))
    attended = merge_windows(attended, images)
    if shifted:
        attended = jnp.roll(attended, (SHIFT, SHIFT), (1, 2))
    middle = field + low_back(jnp.dot(attended, attention_out, precision=highest) + biases[3])
    normed_two = low(norm_rows(middle, norm_gains[1], biases[4]))
    hidden = low_back(jnp.dot(normed_two, up_weight, precision=highest) + up_bias)
    active = low(jax.nn.gelu(hidden, approximate=False))
    return middle + low_back(jnp.dot(active, down_weight, precision=highest) + biases[5])

def block_pair(images, params, present, offset_index, region_bias):
    no_bias = jnp.zeros_like(region_bias)
    first = swin_layer(images, tuple((p[0] for p in params)), False, offset_index, no_bias)
    sent = low_back(low(first))
    return present * swin_layer(sent, tuple((p[1] for p in params)), True, offset_index, region_bias)

def reference(boundary, norm_gains, biases, up_bias, offset_table, attention_in, attention_out, up_weight, down_weight, offset_index, regions, micro_counts):
    weights = tuple((w.astype(jnp.float32) for w in (norm_gains, biases, up_bias, offset_table, attention_in, attention_out, up_weight, down_weight)))
    region_win = split_windows(regions[None, :, :, None]).reshape(WINS, WIN * WIN)
    region_bias = jnp.where(region_win[:, :, None] == region_win[:, None, :], 0.0, -100.0).astype(jnp.float32)
    devices = N_SHARD * N_REPLICA
    inputs = boundary[0].reshape(MB * devices, IMG_MB, SIDE, SIDE, D)
    cotangents = boundary[1].reshape(MB * devices, IMG_MB, SIDE, SIDE, D)
    counts = jnp.repeat(micro_counts, devices)

    def one_group(totals, item):
        images, cotangent, count = item
        present = (jnp.arange(IMG_MB) < count).astype(jnp.float32)[:, None, None, None]
        forward = partial(block_pair, present=present, offset_index=offset_index, region_bias=region_bias)
        output, pullback = jax.vjp(forward, images.astype(jnp.float32), weights)
        grad_in, grad_weights = pullback(cotangent.astype(jnp.float32))
        totals = jax.tree.map(jnp.add, totals, grad_weights)
        return (totals, (output.astype(jnp.bfloat16), grad_in.astype(jnp.bfloat16)))
    zeros = jax.tree.map(jnp.zeros_like, weights)
    totals, pair = lax.scan(one_group, zeros, (inputs, cotangents, counts))
    outputs, grads_in = pair
    results = jnp.stack([grads_in.reshape(boundary.shape[1:]), outputs.reshape(boundary.shape[1:])])
    return (results, totals[0], totals[1], totals[2], totals[3], totals[4], totals[5], totals[6], totals[7])
```

```python
import functools

import jax
import jax.numpy as jnp
import numpy as np
from jax import lax
from jax.experimental import pallas as pl
from jax.experimental.pallas import tpu as pltpu
from jax.sharding import PartitionSpec as P

WIN = 7
SIDE = 14
SHIFT = 3
LEN = WIN * WIN
WINS = 4
SLOT = 64
ROWS = WINS * SLOT
LINE = 16
FRAME = SIDE * LINE
HEADS = 16
QUAD = 4
GROUPS = HEADS // QUAD
WIDE = QUAD * SLOT
F32 = jnp.float32
BF16 = jnp.bfloat16


def window_place(shift):
    place = np.zeros((ROWS, FRAME), np.float32)
    for window in range(WINS):
        for token in range(LEN):
            line = ((window // 2) * WIN + token // WIN + shift) % SIDE
            column = ((window % 2) * WIN + token % WIN + shift) % SIDE
            place[window * SLOT + token, line * LINE + column] = 1.0
    return place


def mm(a, b):
    return jnp.dot(a, b, preferred_element_type=F32)


def mm_nt(a, b):
    return lax.dot_general(a, b, (((1,), (1,)), ((), ())), preferred_element_type=F32)


def mm_tn(a, b):
    return lax.dot_general(a, b, (((0,), (0,)), ((), ())), preferred_element_type=F32)


def standard(v):
    centered = v - jnp.mean(v, -1, keepdims=True)
    spread = jnp.mean(centered * centered, -1, keepdims=True)
    inverse = lax.rsqrt(spread + 1e-05)
    return centered * inverse, inverse


def gelu_pair(h):
    density = jnp.exp(-0.5 * h * h)
    t = 1.0 / (1.0 + (0.3275911 * 0.7071067811865476) * jnp.abs(h))
    poly = t * (
        0.5 * 0.254829592
        + t
        * (
            0.5 * -0.284496736
            + t * (0.5 * 1.421413741 + t * (0.5 * -1.453152027 + t * (0.5 * 1.061405429)))
        )
    )
    tail = poly * density
    cdf = jnp.where(h < 0, tail, 1.0 - tail)
    return h * cdf, cdf + h * (density * 0.3989422804014327)


def head_mask(shape):
    rows = lax.broadcasted_iota(jnp.int32, shape, 0) // SLOT
    lanes = lax.broadcasted_iota(jnp.int32, shape, 1) // 32
    return rows == lanes


def spread_heads(block, mask):
    return jnp.where(mask, jnp.concatenate([block] * QUAD, 0), jnp.zeros((), block.dtype))


def join_heads(blocks):
    lane = lax.broadcasted_iota(jnp.int32, (SLOT, 128), 1) // 32
    out = blocks[:SLOT]
    for h in range(1, QUAD):
        out = jnp.where(lane == h, blocks[h * SLOT : (h + 1) * SLOT], out)
    return out


def weight_copies(info, pieces, places, sems):
    w_in, w_out, w_up, w_down = places
    core, me = info[1], info[2]
    copies = []

    def add(src, dst):
        copies.append(pltpu.make_async_copy(src, dst, sems.at[len(copies)]))

    for half_at in range(2):
        half = core if half_at == 0 else 1 - core
        for shard_at in range(4):
            shard = jnp.bitwise_xor(me, shard_at)
            attn_a, attn_b, mlp_a, mlp_b = pieces[(half_at * 4 + shard_at) * 4 :][:4]
            row = pl.multiple_of(shard * 128 + half * 64, 64)
            add(attn_a.at[0:64], w_in.at[pl.ds(row, 64), 0:512])
            add(attn_a.at[64:128], w_in.at[pl.ds(row, 64), 512:1024])
            add(attn_b.at[0:64], w_in.at[pl.ds(row, 64), 1024:1536])
            add(attn_b.at[64:128], w_out.at[pl.ds(row, 64), :])
            for c in range(4):
                add(mlp_a.at[64 * c : 64 * c + 64], w_up.at[pl.ds(row, 64), 512 * c : 512 * c + 512])
            deep = pl.multiple_of(shard * 512 + half * 256, 256)
            add(mlp_b, w_down.at[pl.ds(deep, 256), :])
    return copies


N_COPIES = 72


def forward_kernel(has_pin, info, *refs):
    pieces, refs = refs[:32], refs[32:]
    x_ref, pin_ref, pout_ref, vec_ref, up_bias_ref, bias_ref, *refs = refs
    out_ref, qkv_ref, p_ref, att_ref, mid_ref, act_ref, slope_ref, *refs = refs
    w_in, w_out, w_up, w_down, sems = refs
    step = pl.program_id(0)

    @pl.when(step == 0)
    def _():
        copies = weight_copies(info, pieces, (w_in, w_out, w_up, w_down), sems)
        for c in copies:
            c.start()
        for c in copies:
            c.wait()

    @pl.when(step < info[0])
    def _():
        x = x_ref[0]
        x = mm(pin_ref[...], x) if has_pin else x.astype(F32)
        xhat, _ = standard(x)
        normed = (xhat * vec_ref[0:1] + vec_ref[2:3]).astype(BF16)
        for part in range(3):
            block = mm(normed, w_in[:, 512 * part : 512 * part + 512])
            if part != 1:
                row = 3 if part == 0 else 4
                block = block + vec_ref[row : row + 1]
            qkv_ref[0, :, 512 * part : 512 * part + 512] = block.astype(BF16)
        mask = head_mask((WIDE, 128))

        def window(w, _):
            rows = pl.ds(pl.multiple_of(w * SLOT, SLOT), SLOT)
            for g in range(GROUPS):
                q = qkv_ref[0, rows, 128 * g : 128 * g + 128]
                k = qkv_ref[0, rows, 512 + 128 * g : 640 + 128 * g]
                v = qkv_ref[0, rows, 1024 + 128 * g : 1152 + 128 * g]
                s = mm_nt(k, spread_heads(q, mask)) * (32**-0.5) + bias_ref[w, g]
                e = jnp.exp(s - jnp.max(s, 0, keepdims=True))
                p = (e * (1.0 / jnp.sum(e, 0, keepdims=True))).astype(BF16)
                p_ref[0, w, g] = p
                att_ref[0, rows, 128 * g : 128 * g + 128] = join_heads(mm_tn(p, v)).astype(BF16)
            return 0

        lax.fori_loop(0, WINS, window, 0)
        mid = x + (mm(att_ref[0], w_out[...]) + vec_ref[5:6])
        mid_ref[0] = mid
        xhat, _ = standard(mid)
        normed_two = (xhat * vec_ref[1:2] + vec_ref[6:7]).astype(BF16)
        down = None
        for c in range(4):
            cols = slice(512 * c, 512 * c + 512)
            hidden = mm(normed_two, w_up[:, cols]) + up_bias_ref[:, cols]
            active, slope = gelu_pair(hidden)
            active = active.astype(BF16)
            act_ref[0, :, cols] = active
            slope_ref[0, :, cols] = slope.astype(BF16)
            part = mm(active, w_down[cols, :])
            down = part if down is None else down + part
        out = (mid + (down + vec_ref[7:8])).astype(BF16)
        out_ref[0] = mm(pout_ref[...], out).astype(BF16)


def backward_kernel(has_xpin, has_gpin, info, *refs):
    pieces, refs = refs[:32], refs[32:]
    g_ref, x_ref, pin_ref, pout_ref, vec_ref, *refs = refs
    qkv_ref, p_ref, att_ref, mid_ref, act_ref, slope_ref, *refs = refs
    gx_ref, mlp_ref, attn_ref, vec_out, up_out, table_out, *refs = refs
    w_in, w_out, w_up, w_down, sems, d_in, d_out, d_up, d_down, gqkv = refs
    step = pl.program_id(0)

    @pl.when(step == 0)
    def _():
        copies = weight_copies(info, pieces, (w_in, w_out, w_up, w_down), sems)
        for c in copies:
            c.start()
        for total in (d_in, d_out, d_up, d_down, vec_out, up_out, table_out):
            total[...] = jnp.zeros(total.shape, F32)
        for c in copies:
            c.wait()

    def add_row(at, value):
        vec_out[at : at + 1] += jnp.sum(value, 0, keepdims=True)

    @pl.when(step < info[0])
    def _():
        g = g_ref[0]
        if has_gpin:
            g = mm(pin_ref[...], g).astype(BF16)
        add_row(7, g.astype(F32))
        xhat_two, inverse_two = standard(mid_ref[0])
        normed_two = (xhat_two * vec_ref[1:2] + vec_ref[6:7]).astype(BF16)
        g_normed = None
        for c in range(4):
            cols = slice(512 * c, 512 * c + 512)
            d_down[:, cols] += mm_tn(g, act_ref[0, :, cols])
            g_hidden = mm_nt(g, w_down[cols, :]) * slope_ref[0, :, cols].astype(F32)
            g_hidden = g_hidden.astype(BF16)
            up_out[:, cols] += jnp.sum(g_hidden.astype(F32), 0, keepdims=True)
            d_up[:, cols] += mm_tn(normed_two, g_hidden)
            part = mm_nt(g_hidden, w_up[:, cols])
            g_normed = part if g_normed is None else g_normed + part

        def norm_back(g_normed, xhat, inverse, gain_row, shift_row, gain):
            add_row(gain_row, g_normed * xhat)
            add_row(shift_row, g_normed)
            u = g_normed * gain
            lean = jnp.mean(u * xhat, -1, keepdims=True)
            return (u - jnp.mean(u, -1, keepdims=True) - xhat * lean) * inverse

        g_middle = g.astype(F32) + norm_back(g_normed, xhat_two, inverse_two, 1, 6, vec_ref[1:2])
        g_update = g_middle.astype(BF16)
        add_row(5, g_update.astype(F32))
        d_out[...] += mm_tn(att_ref[0], g_update)
        g_att = mm_nt(g_update, w_out[...]).astype(BF16)
        gqkv[:, 0:512] = g_att
        mask = head_mask((WIDE, 128))

        def window(w, _):
            rows = pl.ds(pl.multiple_of(w * SLOT, SLOT), SLOT)
            for h in range(GROUPS):
                q = qkv_ref[0, rows, 128 * h : 128 * h + 128]
                k = qkv_ref[0, rows, 512 + 128 * h : 640 + 128 * h]
                v = qkv_ref[0, rows, 1024 + 128 * h : 1152 + 128 * h]
                p = p_ref[0, w, h]
                g_out = spread_heads(gqkv[rows, 128 * h : 128 * h + 128], mask)
                g_v = mm(p, g_out)
                pf = p.astype(F32)
                g_p = mm_nt(v, g_out)
                g_s = pf * (g_p - jnp.sum(pf * g_p, 0, keepdims=True))
                g_s = g_s.astype(BF16)
                table_out[h] += g_s.astype(F32)
                g_k = mm(g_s, spread_heads(q, mask)) * (32**-0.5)
                g_q = join_heads(mm_tn(g_s, k)) * (32**-0.5)
                gqkv[rows, 128 * h : 128 * h + 128] = g_q.astype(BF16)
                gqkv[rows, 512 + 128 * h : 640 + 128 * h] = g_k.astype(BF16)
                gqkv[rows, 1024 + 128 * h : 1152 + 128 * h] = g_v.astype(BF16)
            return 0

        lax.fori_loop(0, WINS, window, 0)
        x = x_ref[0]
        x = mm(pin_ref[...], x) if has_xpin else x.astype(F32)
        xhat, inverse = standard(x)
        normed = (xhat * vec_ref[0:1] + vec_ref[2:3]).astype(BF16)
        g_normed = None
        for part in range(3):
            cols = slice(512 * part, 512 * part + 512)
            block = gqkv[:, cols]
            d_in[:, cols] += mm_tn(normed, block)
            if part != 1:
                add_row(3 if part == 0 else 4, block.astype(F32))
            term = mm_nt(block, w_in[:, cols])
            g_normed = term if g_normed is None else g_normed + term
        g_field = g_middle + norm_back(g_normed, xhat, inverse, 0, 2, vec_ref[0:1])
        gx_ref[0] = mm(pout_ref[...], g_field.astype(BF16)).astype(BF16)

    @pl.when(step == pl.num_programs(0) - 1)
    def _():
        core, me = info[1], info[2]
        for half in range(2):
            half_at = jnp.bitwise_xor(core, half)
            for shard in range(4):
                at = jnp.bitwise_xor(me, shard)
                top = 128 * shard + 64 * half
                for c in range(3):
                    attn_ref[half_at, at, 64 * c : 64 * c + 64, :] = d_in[
                        top : top + 64, 512 * c : 512 * c + 512
                    ].astype(BF16)
                attn_ref[half_at, at, 192:256, :] = d_out[top : top + 64, :].astype(BF16)
                for c in range(4):
                    mlp_ref[half_at, at, 64 * c : 64 * c + 64, :] = d_up[
                        top : top + 64, 512 * c : 512 * c + 512
                    ].astype(BF16)
                deep = 512 * shard + 256 * half
                mlp_ref[half_at, at, 256:512, :] = d_down[:, deep : deep + 256].T.astype(BF16)


def whole(shape):
    return pl.BlockSpec(shape, lambda i, info: (0,) * len(shape))


def each(shape):
    return pl.BlockSpec(
        (1,) + shape,
        lambda i, info: (jnp.maximum(jnp.minimum(i, info[0] - 1), 0),) + (0,) * len(shape),
    )


SAVED = (
    ((ROWS, 1536), BF16),
    ((WINS, GROUPS, SLOT, WIDE), BF16),
    ((ROWS, 512), BF16),
    ((ROWS, 512), F32),
    ((ROWS, 2048), BF16),
    ((ROWS, 2048), BF16),
)
WEIGHTS = [
    pltpu.VMEM((512, 1536), BF16),
    pltpu.VMEM((512, 512), BF16),
    pltpu.VMEM((512, 2048), BF16),
    pltpu.VMEM((2048, 512), BF16),
    pltpu.SemaphoreType.DMA((N_COPIES,)),
]
PARAMS = pltpu.CompilerParams(vmem_limit_bytes=58 * 1024 * 1024)


def run_forward(info, pieces, x, pin, pout, vec, up_bias, bias):
    count = x.shape[0]
    out_rows = pout.shape[0]
    saved = [each(shape) for shape, _ in SAVED]
    return pl.pallas_call(
        functools.partial(forward_kernel, pin is not None),
        grid_spec=pltpu.PrefetchScalarGridSpec(
            num_scalar_prefetch=1,
            grid=(count,),
            in_specs=[pl.BlockSpec(memory_space=pl.ANY)] * 32
            + [
                each(x.shape[1:]),
                whole((ROWS, FRAME)),
                whole(pout.shape),
                whole(vec.shape),
                whole(up_bias.shape),
                whole(bias.shape),
            ],
            out_specs=[each((out_rows, 512))] + saved,
            scratch_shapes=WEIGHTS,
        ),
        out_shape=[jax.ShapeDtypeStruct((count, out_rows, 512), BF16)]
        + [jax.ShapeDtypeStruct((count,) + shape, kind) for shape, kind in SAVED],
        compiler_params=PARAMS,
    )(
        info,
        *pieces,
        x,
        jnp.zeros((ROWS, FRAME), BF16) if pin is None else pin,
        pout,
        vec,
        up_bias,
        bias,
    )


def run_backward(info, pieces, g, x, pin, pout, vec, saved):
    count = x.shape[0]
    out_rows = pout.shape[0]
    x_framed = x.shape[1] == FRAME
    g_framed = g.shape[1] == FRAME
    return pl.pallas_call(
        functools.partial(backward_kernel, x_framed, g_framed),
        grid_spec=pltpu.PrefetchScalarGridSpec(
            num_scalar_prefetch=1,
            grid=(count,),
            in_specs=[pl.BlockSpec(memory_space=pl.ANY)] * 32
            + [
                each(g.shape[1:]),
                each(x.shape[1:]),
                whole(pin.shape),
                whole(pout.shape),
                whole(vec.shape),
            ]
            + [each(shape) for shape, _ in SAVED],
            out_specs=[
                each((out_rows, 512)),
                whole((2, 4, 512, 512)),
                whole((2, 4, 256, 512)),
                whole((8, 512)),
                whole((1, 2048)),
                whole((GROUPS, SLOT, WIDE)),
            ],
            scratch_shapes=WEIGHTS
            + [
                pltpu.VMEM((512, 1536), F32),
                pltpu.VMEM((512, 512), F32),
                pltpu.VMEM((512, 2048), F32),
                pltpu.VMEM((512, 2048), F32),
                pltpu.VMEM((ROWS, 1536), BF16),
            ],
        ),
        out_shape=[
            jax.ShapeDtypeStruct((count, out_rows, 512), BF16),
            jax.ShapeDtypeStruct((2, 4, 512, 512), BF16),
            jax.ShapeDtypeStruct((2, 4, 256, 512), BF16),
            jax.ShapeDtypeStruct((8, 512), F32),
            jax.ShapeDtypeStruct((1, 2048), F32),
            jax.ShapeDtypeStruct((GROUPS, SLOT, WIDE), F32),
        ],
        compiler_params=PARAMS,
    )(info, *pieces, g, x, pin, pout, vec, *saved)


def swap(block):
    return lax.ppermute(block, "section", [(0, 1), (1, 0)])


def across(block, bit):
    return lax.ppermute(block, "shard", [(i, i ^ bit) for i in range(4)])


def gather_chunk(a, b):
    xa, xb, ya, yb = across(a, 1), across(b, 1), across(a, 2), across(b, 2)
    da, db = across(xa, 2), across(yb, 1)
    mine = [(a, b), (xa, xb), (ya, yb), (da, db)]
    other = [(swap(p), swap(q)) for p, q in mine]
    return mine + other


def add_low(*terms):
    total = terms[0].astype(F32)
    for term in terms[1:]:
        total = total + term.astype(F32)
    return total.astype(BF16)


def reduce_chunk(block):
    rows = block.shape[2]
    low, high = slice(0, rows // 2), slice(rows // 2, rows)
    total = add_low(block[0], swap(block[1]))
    x_low, y_high = across(total[1, low], 1), across(total[2, high], 2)
    to_y = across(total[3, low], 1)
    to_x = across(total[3, high], 2)
    x_high = across(add_low(total[1, high], to_x), 1)
    y_low = across(add_low(total[2, low], to_y), 2)
    x_sum = jnp.concatenate([x_low, x_high], 0)
    y_sum = jnp.concatenate([y_low, y_high], 0)
    owned = add_low(total[0], x_sum, y_sum)
    return replica_sum(owned)


def replica_sum(owned):
    size = lax.axis_size("replica")
    if size != 4:
        return lax.psum(owned, "replica")
    at = lax.axis_index("replica")
    quarters = owned.reshape(4, -1, 512)

    def distance(block, bit):
        return lax.ppermute(block, "replica", [(i, i ^ bit) for i in range(4)])

    def pick(bit):
        return lax.dynamic_index_in_dim(quarters, at ^ bit, 0, keepdims=False)

    total = add_low(pick(0), *[distance(pick(bit), bit) for bit in (1, 2, 3)])
    held = [total] + [distance(total, bit) for bit in (1, 2, 3)]
    ordered = jnp.zeros_like(quarters)
    for bit in range(4):
        ordered = lax.dynamic_update_index_in_dim(ordered, held[bit], at ^ bit, 0)
    return ordered.reshape(owned.shape)


def body(
    boundary,
    norm_gains,
    biases,
    up_bias,
    offset_table,
    attention_in,
    attention_out,
    up_weight,
    down_weight,
    offset_index,
    regions,
    micro_counts,
):
    core = lax.axis_index("section")
    first = core == 0
    me = lax.axis_index("shard")
    mb_count, per_device = boundary.shape[1], boundary.shape[2]
    slots = mb_count * per_device
    share = (slots + 1) // 2

    present = (jnp.arange(per_device)[None] < micro_counts[:, None]).reshape(slots)
    rank = jnp.cumsum(present.astype(jnp.int32)) - 1
    owner = jnp.bitwise_and(rank, 1)
    place = jnp.right_shift(rank, 1)

    def slots_of(whose):
        hit = present & (owner == whose)
        hit = hit[None] & (place[None] == jnp.arange(share)[:, None])
        return jnp.sum(jnp.where(hit, jnp.arange(slots)[None], 0), 1)

    total_images = jnp.sum(present.astype(jnp.int32))
    own_count = jnp.right_shift(total_images + 1 - core, 1)
    info = jnp.stack([own_count, core, me]).astype(jnp.int32)

    framed = jnp.pad(
        boundary.reshape(slots, SIDE, SIDE, 512), ((0, 0), (0, 0), (0, LINE - SIDE), (0, 0))
    ).reshape(slots, FRAME, 512)
    kept = framed[slots_of(core)]
    other = swap(framed[slots_of(1 - core)])
    images = jnp.where(first, kept, other)
    cotangents = jnp.where(first, other, kept)

    def halves(block, rows):
        return block.reshape(2, rows, 512)

    def columns(weight):
        rows, cols = weight.shape
        return weight.reshape(2, rows // 2, cols // 512, 512).transpose(0, 2, 1, 3)

    w_in, w_out = columns(attention_in[0]), columns(attention_out[0])
    w_up = columns(up_weight[0])
    parts = [
        w_in[:, 0:2].reshape(2, 128, 512),
        jnp.concatenate([w_in[:, 2], w_out[:, 0]], 1),
        w_up.reshape(2, 256, 512),
        down_weight[0].reshape(2, 256, 512),
    ]
    pieces = [[], []]
    own_parts, other_parts = [], []
    for part in parts:
        keep = jnp.where(first, part[0], part[1])
        give = jnp.where(first, part[1], part[0])
        got = swap(give)
        own_parts.append(keep)
        other_parts.append(got)
    for layer in range(2):
        mine = [
            jnp.where(core == layer, keep, got) for keep, got in zip(own_parts, other_parts)
        ]
        attn = gather_chunk(mine[0], mine[1])
        mlp = gather_chunk(mine[2], mine[3])
        for (a, b), (c, d) in zip(attn, mlp):
            pieces[layer] += [a, b, c, d]

    flat = jnp.concatenate(
        [
            norm_gains[0].reshape(-1),
            biases[0].reshape(-1),
            up_bias[0].reshape(-1),
            offset_table[0].reshape(-1),
        ]
    )
    small = lax.all_gather(flat, ("section", "shard"), axis=0, tiled=False)
    small = small.reshape(2, 4, -1).astype(F32)
    rel = offset_table.shape[1]
    gains = small[:, :, 0:256].reshape(2, 4, 2, 128).transpose(0, 2, 1, 3).reshape(2, 2, 512)
    shifts = small[:, :, 256:1024].reshape(2, 4, 6, 128).transpose(0, 2, 1, 3).reshape(2, 6, 512)
    vecs = jnp.concatenate([gains, shifts], 1)
    lifts = small[:, :, 1024:1536].reshape(2, 1, 2048)
    tables = small[:, :, 1536:].reshape(2, 4, rel, 4).transpose(0, 2, 1, 3).reshape(2, rel, HEADS)

    onehot = (offset_index.T.reshape(-1)[:, None] == jnp.arange(rel)[None, :]).astype(BF16)
    split = regions.reshape(2, WIN, 2, WIN).transpose(0, 2, 1, 3).reshape(WINS, LEN)
    apart = jnp.where(split[:, :, None] == split[:, None, :], 0.0, -100.0).astype(F32)
    bias = []
    for layer in range(2):
        offsets = jnp.dot(onehot, tables[layer].astype(BF16), preferred_element_type=F32)
        offsets = offsets.reshape(LEN, LEN, GROUPS, QUAD).transpose(2, 0, 3, 1)
        full = jnp.broadcast_to(offsets[None], (WINS,) + offsets.shape)
        if layer == 1:
            full = full + apart.transpose(0, 2, 1)[:, None, :, None, :]
        full = jnp.pad(full, ((0, 0),) * 4 + ((0, SLOT - LEN),))
        full = jnp.pad(full, ((0, 0),) * 2 + ((0, SLOT - LEN),) + ((0, 0),) * 2, constant_values=-1e30)
        bias.append(full.reshape(WINS, GROUPS, SLOT, WIDE))

    plain, moved = window_place(0), window_place(SHIFT)
    to_plain, to_moved = jnp.asarray(plain, BF16), jnp.asarray(moved, BF16)
    plain_moved = jnp.asarray(moved @ plain.T, BF16)

    sent, *saved_one = run_forward(
        info, pieces[0], images, to_plain, plain_moved, vecs[0], lifts[0], bias[0]
    )
    output, *saved_two = run_forward(
        info, pieces[1], sent, None, to_moved.T, vecs[1], lifts[1], bias[1]
    )
    g_sent, mlp_two, attn_two, *small_two = run_backward(
        info, pieces[1], cotangents, sent, to_moved, plain_moved.T, vecs[1], saved_two
    )
    g_image, mlp_one, attn_one, *small_one = run_backward(
        info, pieces[0], g_sent, images, to_plain, to_plain.T, vecs[0], saved_one
    )

    big = []
    for mlp, attn in ((mlp_one, attn_one), (mlp_two, attn_two)):
        big.append(jnp.concatenate([reduce_chunk(attn), reduce_chunk(mlp)], 0))
    hold = jnp.where(first, big[0], big[1])
    back = swap(jnp.where(first, big[1], big[0]))
    both = jnp.stack([jnp.where(first, hold, back), jnp.where(first, back, hold)]).astype(F32)
    grad_in = both[:, 0:192].reshape(2, 3, 64, 512).transpose(0, 2, 1, 3).reshape(128, 1536)
    grad_out = both[:, 192:256].reshape(128, 512)
    grad_up = both[:, 256:512].reshape(2, 4, 64, 512).transpose(0, 2, 1, 3).reshape(128, 2048)
    grad_down = both[:, 512:768].reshape(512, 512)

    pairs = offset_index.T.reshape(-1)
    match = (pairs[None, :] == jnp.arange(rel)[:, None]).astype(F32)
    bundle = []
    for vec, up, table in (small_one, small_two):
        table = table.reshape(GROUPS, SLOT, QUAD, SLOT)[:, :LEN, :, :LEN]
        table = table.transpose(1, 3, 0, 2).reshape(LEN * LEN, HEADS)
        table = jnp.dot(match, table, precision=lax.Precision.HIGHEST)
        bundle.append(jnp.concatenate([vec.reshape(-1), up.reshape(-1), table.reshape(-1)]))
    bundle = jnp.stack(bundle).astype(BF16)
    bundle = lax.psum(bundle, ("section", "shard", "replica")).astype(F32)
    bundle = lax.dynamic_index_in_dim(bundle, core, 0, keepdims=False)
    vec = lax.dynamic_slice_in_dim(bundle[:4096].reshape(8, 512), me * 128, 128, 1)
    grad_lift = lax.dynamic_slice_in_dim(bundle[4096:6144], me * 512, 512, 0)
    grad_table = lax.dynamic_slice_in_dim(bundle[6144:].reshape(rel, HEADS), me * 4, 4, 1)

    hold = jnp.where(first, g_image, output)
    back = swap(jnp.where(first, output, g_image))
    every = jnp.concatenate([hold, back], 0)
    source = jnp.clip(jnp.where(owner == core, 0, share) + place, 0, 2 * share - 1)
    chosen = every[source].reshape(slots, SIDE, LINE, 512)[:, :, :SIDE]
    chosen = jnp.where(present[:, None, None, None], chosen, jnp.zeros((), BF16))
    results = chosen.reshape(1, mb_count, per_device, SIDE, SIDE, 512)
    return (
        results,
        vec[None, 0:2],
        vec[None, 2:8],
        grad_lift[None],
        grad_table[None],
        grad_in[None],
        grad_out[None],
        grad_up[None],
        grad_down[None],
    )


def solution(mesh):
    placed = (
        P("section", None, ("shard", "replica"), None, None, None),
        P("section", None, "shard"),
        P("section", None, "shard"),
        P("section", "shard"),
        P("section", None, "shard"),
        P("section", "shard", None),
        P("section", "shard", None),
        P("section", "shard", None),
        P("section", "shard", None),
        P(),
        P(),
        P(),
    )
    return jax.shard_map(
        body,
        mesh=mesh,
        in_specs=placed,
        out_specs=(placed[0],) + placed[1:9],
        check_vma=False,
    )
```

```python
import functools

import jax
import jax.numpy as jnp
import numpy as np
from jax import lax
from jax.experimental import pallas as pl
from jax.experimental.pallas import tpu as pltpu
from jax.sharding import PartitionSpec as P

WIN = 7
SIDE = 14
SHIFT = 3
LEN = WIN * WIN
WINS = 4
SLOT = 64
ROWS = WINS * SLOT
TOKENS = SIDE * SIDE
FRAME = 208
HEADS = 16
QUAD = 4
GROUPS = HEADS // QUAD
WIDE = QUAD * SLOT
LOG2E = 1.4426950408889634
F32 = jnp.float32
BF16 = jnp.bfloat16


def window_place(shift):
    place = np.zeros((ROWS, FRAME), np.float32)
    for window in range(WINS):
        for token in range(LEN):
            line = ((window // 2) * WIN + token // WIN + shift) % SIDE
            column = ((window % 2) * WIN + token % WIN + shift) % SIDE
            place[window * SLOT + token, line * SIDE + column] = 1.0
    return place


def mm(a, b):
    return jnp.dot(a, b, preferred_element_type=F32)


def mm_nt(a, b):
    return lax.dot_general(a, b, (((1,), (1,)), ((), ())), preferred_element_type=F32)


def mm_tn(a, b):
    return lax.dot_general(a, b, (((0,), (0,)), ((), ())), preferred_element_type=F32)


def standard(v):
    centered = v - jnp.mean(v, -1, keepdims=True)
    spread = jnp.mean(centered * centered, -1, keepdims=True)
    inverse = lax.rsqrt(spread + 1e-05)
    return centered * inverse, inverse


def gelu_pair(h):
    density = jnp.exp(-0.5 * h * h)
    t = 1.0 / (1.0 + (0.3275911 * 0.7071067811865476) * jnp.abs(h))
    poly = t * (
        0.5 * 0.254829592
        + t
        * (
            0.5 * -0.284496736
            + t * (0.5 * 1.421413741 + t * (0.5 * -1.453152027 + t * (0.5 * 1.061405429)))
        )
    )
    tail = poly * density
    cdf = jnp.where(h < 0, tail, 1.0 - tail)
    return h * cdf, cdf + h * (density * 0.3989422804014327)


def head_mask(shape):
    rows = lax.broadcasted_iota(jnp.int32, shape, 0) // SLOT
    lanes = lax.broadcasted_iota(jnp.int32, shape, 1) // 32
    return rows == lanes


def spread_heads(block, mask):
    return jnp.where(mask, jnp.concatenate([block] * QUAD, 0), jnp.zeros((), block.dtype))


def join_heads(blocks):
    lane = lax.broadcasted_iota(jnp.int32, (SLOT, 128), 1) // 32
    out = blocks[:SLOT]
    for h in range(1, QUAD):
        out = jnp.where(lane == h, blocks[h * SLOT : (h + 1) * SLOT], out)
    return out


def attn_load(layer, info, pieces, w_in, sems, clear=()):
    mine, other = pieces

    def copies(source):
        pairs = []
        for at in range(4):
            row = pl.multiple_of(jnp.bitwise_xor(info[2], at) * 128, 128)
            for c in range(3):
                src = source.at[at, 128 * c : 128 * c + 128]
                pairs.append((src, w_in.at[pl.ds(row, 128), 512 * c : 512 * c + 512]))
        return [pltpu.make_async_copy(*pair, sems.at[n]) for n, pair in enumerate(pairs)]

    @pl.when(pl.program_id(0) == 0)
    def _():
        @pl.when(info[1] == layer)
        def _():
            for c in copies(mine):
                c.start()

        @pl.when(info[1] != layer)
        def _():
            for c in copies(other):
                c.start()

        for total in clear:
            total[...] = jnp.zeros(total.shape, F32)
        for c in copies(mine):
            c.wait()


def mlp_copies(info, pieces, places, sems):
    w_out, w_up, w_down = places
    copies = []
    for half_at in range(2):
        half = jnp.bitwise_xor(info[1], half_at)
        for shard_at in range(4):
            shard = jnp.bitwise_xor(info[2], shard_at)
            piece = pieces[4].at[shard_at] if half_at else pieces[shard_at]
            row = pl.multiple_of(shard * 128 + half * 64, 64)
            deep = pl.multiple_of(shard * 512 + half * 256, 256)
            pairs = [
                (piece.at[64 * c : 64 * c + 64], w_up.at[pl.ds(row, 64), 512 * c : 512 * c + 512])
                for c in range(4)
            ]
            pairs.append((piece.at[256:512], w_down.at[pl.ds(deep, 256), :]))
            pairs.append((piece.at[512:576], w_out.at[pl.ds(row, 64), :]))
            for src, dst in pairs:
                copies.append(pltpu.make_async_copy(src, dst, sems.at[len(copies)]))
    return copies


def group_lanes(g):
    return lambda part: slice(512 * part + 128 * g, 512 * part + 128 * g + 128)


BLOCKS = [
    (w, slice(w * SLOT, w * SLOT + SLOT), g, group_lanes(g))
    for w in range(WINS)
    for g in range(GROUPS)
]


def load_weights(copies, clear=()):
    @pl.when(pl.program_id(0) == 0)
    def _():
        for c in copies:
            c.start()
        for total in clear:
            total[...] = jnp.zeros(total.shape, F32)
        for c in copies:
            c.wait()


def attn_forward_kernel(layer, info, *refs):
    pieces, refs = refs[:2], refs[2:]
    x_ref, cut_ref, join_ref, vec_ref, bias_ref, apart_ref, *refs = refs
    qkv_ref, p_ref, att_ref, w_in, sems, att = refs
    attn_load(layer, info, pieces, w_in, sems)

    @pl.when(pl.program_id(0) < info[0])
    def _():
        xhat, _ = standard(x_ref[0].astype(F32))
        normed = (xhat * vec_ref[0:1] + vec_ref[2:3]).astype(BF16)
        normed = mm(cut_ref[...], normed).astype(BF16)
        for part in range(3):
            block = mm(normed, w_in[:, 512 * part : 512 * part + 512])
            if part != 1:
                row = 3 if part == 0 else 4
                block = block + vec_ref[row : row + 1]
            qkv_ref[0, :, 512 * part : 512 * part + 512] = block.astype(BF16)
        mask = head_mask((WIDE, 128))
        factor = 32**-0.5 * LOG2E

        scores, probs, outs = [], [], []
        for w, rows, g, lanes in BLOCKS:
            q = qkv_ref[0, rows, lanes(0)]
            bias = bias_ref[g] + apart_ref[w] if layer else bias_ref[g]
            scores.append(mm_nt(qkv_ref[0, rows, lanes(1)], spread_heads(q, mask)) * factor + bias)
        for s in scores:
            e = jnp.exp2(s - jnp.max(s, 0, keepdims=True))
            probs.append((e * (1.0 / jnp.sum(e, 0, keepdims=True))).astype(BF16))
        for p, (w, rows, g, lanes) in zip(probs, BLOCKS):
            outs.append(mm_tn(p, qkv_ref[0, rows, lanes(2)]))
        for p, out, (w, rows, g, lanes) in zip(probs, outs, BLOCKS):
            p_ref[0, w, g] = p
            att[rows, lanes(0)] = join_heads(out).astype(BF16)
        att_ref[0] = mm(join_ref[...], att[...]).astype(BF16)


def mlp_forward_kernel(info, *refs):
    pieces, refs = refs[:5], refs[5:]
    x_ref, att_ref, vec_ref, up_bias_ref, *refs = refs
    out_ref, mid_ref, act_ref, slope_ref, w_out, w_up, w_down, sems = refs
    load_weights(mlp_copies(info, pieces, (w_out, w_up, w_down), sems))

    @pl.when(pl.program_id(0) < info[0])
    def _():
        mid = x_ref[0].astype(F32) + (mm(att_ref[0], w_out[...]) + vec_ref[5:6])
        mid_ref[0] = mid
        xhat, _ = standard(mid)
        normed_two = (xhat * vec_ref[1:2] + vec_ref[6:7]).astype(BF16)
        cols = [slice(512 * c, 512 * c + 512) for c in range(4)]

        def lift(c):
            return mm(normed_two, w_up[:, cols[c]]) + up_bias_ref[:, cols[c]]

        hidden, active, down = lift(0), None, 0.0
        for c in range(4):
            after = lift(c + 1) if c < 3 else None
            before, (active, slope) = active, gelu_pair(hidden)
            active = active.astype(BF16)
            act_ref[0, :, cols[c]] = active
            slope_ref[0, :, cols[c]] = slope.astype(BF16)
            if c:
                down = down + mm(before, w_down[cols[c - 1], :])
            hidden = after
        down = down + mm(active, w_down[cols[3], :])
        out_ref[0] = (mid + (down + vec_ref[7:8])).astype(BF16)


def add_row(total, at, value):
    total[at : at + 1] += jnp.sum(value, 0, keepdims=True)


def norm_back(total, rows, g_normed, xhat, inverse, gain):
    add_row(total, rows[0], g_normed * xhat)
    add_row(total, rows[1], g_normed)
    u = g_normed * gain
    lean = jnp.mean(u * xhat, -1, keepdims=True)
    return (u - jnp.mean(u, -1, keepdims=True) - xhat * lean) * inverse


def mlp_backward_kernel(info, *refs):
    pieces, refs = refs[:5], refs[5:]
    g_ref, att_ref, mid_ref, act_ref, slope_ref, vec_ref, *refs = refs
    g_mid_ref, g_att_ref, keep_ref, give_ref, vec_out, up_out, *refs = refs
    w_out, w_up, w_down, sems, d_out, d_up, d_down = refs
    load_weights(
        mlp_copies(info, pieces, (w_out, w_up, w_down), sems),
        (d_out, d_up, d_down, vec_out, up_out),
    )

    @pl.when(pl.program_id(0) < info[0])
    def _():
        g = g_ref[0]
        add_row(vec_out, 7, g.astype(F32))
        xhat, inverse = standard(mid_ref[0])
        normed_two = (xhat * vec_ref[1:2] + vec_ref[6:7]).astype(BF16)
        cols = [slice(512 * c, 512 * c + 512) for c in range(4)]
        g_hidden = []
        for c in cols:
            part = (mm_nt(g, w_down[c, :]) * slope_ref[0, :, c].astype(F32)).astype(BF16)
            up_out[:, c] += jnp.sum(part.astype(F32), 0, keepdims=True)
            g_hidden.append(part)
        g_normed = sum(mm_nt(part, w_up[:, c]) for part, c in zip(g_hidden, cols))
        for part, c in zip(g_hidden, cols):
            d_down[:, c] += mm_tn(g, act_ref[0, :, c])
            d_up[:, c] += mm_tn(normed_two, part)
        g_mid = g.astype(F32) + norm_back(vec_out, (1, 6), g_normed, xhat, inverse, vec_ref[1:2])
        g_mid_ref[0] = g_mid
        g_update = g_mid.astype(BF16)
        add_row(vec_out, 5, g_update.astype(F32))
        d_out[...] += mm_tn(att_ref[0], g_update)
        g_att_ref[0] = mm_nt(g_update, w_out[...]).astype(BF16)

    @pl.when(pl.program_id(0) == pl.num_programs(0) - 1)
    def _():
        for out_ref, half in ((keep_ref, info[1]), (give_ref, 1 - info[1])):
            for shard in range(4):
                at = jnp.bitwise_xor(info[2], shard)
                rows = pl.ds(pl.multiple_of(128 * shard + 64 * half, 64), 64)
                for c in range(4):
                    out_ref[at, 64 * c : 64 * c + 64, :] = d_up[
                        rows, 512 * c : 512 * c + 512
                    ].astype(BF16)
                deep = pl.ds(pl.multiple_of(512 * shard + 256 * half, 256), 256)
                out_ref[at, 256:512, :] = d_down[:, deep].T.astype(BF16)
                out_ref[at, 512:576, :] = d_out[rows, :].astype(BF16)


def attn_backward_kernel(layer, info, *refs):
    pieces, refs = refs[:2], refs[2:]
    g_mid_ref, g_att_ref, x_ref, qkv_ref, p_ref, cut_ref, join_ref, vec_ref, *refs = refs
    gx_ref, keep_ref, give_ref, vec_out, table_out, *refs = refs
    w_in, sems, d_in, g_att, gqkv = refs
    attn_load(layer, info, pieces, w_in, sems, (d_in, vec_out, table_out))

    @pl.when(pl.program_id(0) < info[0])
    def _():
        g_att[...] = mm(cut_ref[...], g_att_ref[0]).astype(BF16)
        mask = head_mask((WIDE, 128))

        at = range(len(BLOCKS))
        q, k, v = [[qkv_ref[0, rows, lanes(n)] for _, rows, _, lanes in BLOCKS] for n in range(3)]
        p = [p_ref[0, w, h] for w, _, h, _ in BLOCKS]
        g_out = [spread_heads(g_att[rows, lanes(0)], mask) for _, rows, _, lanes in BLOCKS]
        g_p = [mm_nt(v[n], g_out[n]) for n in at]
        g_v = [mm(p[n], g_out[n]) for n in at]
        g_s = []
        for n in at:
            soft = p[n].astype(F32)
            part = soft * g_p[n]
            g_s.append((part - soft * jnp.sum(part, 0, keepdims=True)).astype(BF16))
        g_k = [mm(g_s[n], spread_heads(q[n], mask)) for n in at]
        g_q = [mm_tn(g_s[n], k[n]) for n in at]
        for n, (_, rows, _, lanes) in enumerate(BLOCKS):
            gqkv[rows, lanes(0)] = (join_heads(g_q[n]) * 32**-0.5).astype(BF16)
            gqkv[rows, lanes(1)] = (g_k[n] * 32**-0.5).astype(BF16)
            gqkv[rows, lanes(2)] = g_v[n].astype(BF16)
        for h in range(GROUPS):
            table_out[h] += sum(g_s[n].astype(F32) for n in at if BLOCKS[n][2] == h)
        xhat, inverse = standard(x_ref[0].astype(F32))
        normed = (xhat * vec_ref[0:1] + vec_ref[2:3]).astype(BF16)
        g_normed = None
        for part in range(3):
            cols = slice(512 * part, 512 * part + 512)
            block = mm(join_ref[...], gqkv[:, cols]).astype(BF16)
            d_in[:, cols] += mm_tn(normed, block)
            if part != 1:
                add_row(vec_out, 3 if part == 0 else 4, block.astype(F32))
            term = mm_nt(block, w_in[:, cols])
            g_normed = term if g_normed is None else g_normed + term
        back = norm_back(vec_out, (0, 2), g_normed, xhat, inverse, vec_ref[0:1])
        gx_ref[0] = (g_mid_ref[0] + back).astype(BF16)

    @pl.when(pl.program_id(0) == pl.num_programs(0) - 1)
    def _():
        for out_ref, half in ((keep_ref, info[1]), (give_ref, 1 - info[1])):
            for shard in range(4):
                at = jnp.bitwise_xor(info[2], shard)
                rows = pl.ds(pl.multiple_of(128 * shard + 64 * half, 64), 64)
                for c in range(3):
                    out_ref[at, 64 * c : 64 * c + 64, :] = d_in[
                        rows, 512 * c : 512 * c + 512
                    ].astype(BF16)


def whole(shape):
    return pl.BlockSpec(shape, lambda i, info: (0,) * len(shape))


def each(shape):
    return pl.BlockSpec(
        (1,) + shape,
        lambda i, info: (jnp.maximum(jnp.minimum(i, info[0] - 1), 0),) + (0,) * len(shape),
    )


X = ((FRAME, 512), BF16)
QKV = ((ROWS, 1536), BF16)
PROB = ((WINS, GROUPS, SLOT, WIDE), BF16)
MID = ((FRAME, 512), F32)
WIDE_X = ((FRAME, 2048), BF16)
VEC = ((8, 512), F32)
ATTN_WEIGHTS = [pltpu.VMEM((512, 1536), BF16), pltpu.SemaphoreType.DMA((12,))]
MLP_WEIGHTS = [
    pltpu.VMEM((512, 512), BF16),
    pltpu.VMEM((512, 2048), BF16),
    pltpu.VMEM((2048, 512), BF16),
    pltpu.SemaphoreType.DMA((48,)),
]


def run(kernel, info, pieces, by_image, shared, outs, shared_outs, scratch, micros):
    count = by_image[0].shape[0]
    return pl.pallas_call(
        kernel,
        grid_spec=pltpu.PrefetchScalarGridSpec(
            num_scalar_prefetch=1,
            grid=(count,),
            in_specs=[pl.BlockSpec(memory_space=pl.ANY)] * len(pieces)
            + [each(a.shape[1:]) for a in by_image]
            + [whole(a.shape) for a in shared],
            out_specs=[each(shape) for shape, _ in outs]
            + [whole(shape) for shape, _ in shared_outs],
            scratch_shapes=scratch,
        ),
        out_shape=[jax.ShapeDtypeStruct((count,) + shape, kind) for shape, kind in outs]
        + [jax.ShapeDtypeStruct(shape, kind) for shape, kind in shared_outs],
        compiler_params=pltpu.CompilerParams(vmem_limit_bytes=56 * 1024 * 1024),
        cost_estimate=pl.CostEstimate(
            flops=int(micros * 1e9), bytes_accessed=int(micros * 1e6), transcendentals=0
        ),
    )(info, *pieces, *by_image, *shared)


def attn_forward(layer, info, pieces, x, cut, join, vec, bias, apart):
    return run(
        functools.partial(attn_forward_kernel, layer),
        info,
        pieces,
        [x],
        [cut, join, vec, bias, apart],
        [QKV, PROB, X],
        [],
        ATTN_WEIGHTS + [pltpu.VMEM((ROWS, 512), BF16)],
        20,
    )


def mlp_forward(info, pieces, x, att, vec, up_bias):
    return run(
        mlp_forward_kernel,
        info,
        pieces,
        [x, att],
        [vec, up_bias],
        [X, MID, WIDE_X, WIDE_X],
        [],
        MLP_WEIGHTS,
        20,
    )


def mlp_backward(info, pieces, g, att, mid, act, slope, vec):
    return run(
        mlp_backward_kernel,
        info,
        pieces,
        [g, att, mid, act, slope],
        [vec],
        [MID, X],
        [((4, 576, 512), BF16)] * 2 + [VEC, ((1, 2048), F32)],
        MLP_WEIGHTS
        + [pltpu.VMEM((512, 512), F32), pltpu.VMEM((512, 2048), F32), pltpu.VMEM((512, 2048), F32)],
        30,
    )


def attn_backward(layer, info, pieces, g_mid, g_att, x, qkv, p, cut, join, vec):
    return run(
        functools.partial(attn_backward_kernel, layer),
        info,
        pieces,
        [g_mid, g_att, x, qkv, p],
        [cut, join, vec],
        [X],
        [((4, 192, 512), BF16)] * 2 + [VEC, ((GROUPS, SLOT, WIDE), F32)],
        ATTN_WEIGHTS
        + [
            pltpu.VMEM((512, 1536), F32),
            pltpu.VMEM((ROWS, 512), BF16),
            pltpu.VMEM((ROWS, 1536), BF16),
        ],
        30,
    )


def swap(block):
    return lax.ppermute(block, "section", [(0, 1), (1, 0)])


def across(block, distance):
    return lax.ppermute(block, "shard", [(i, i ^ distance) for i in range(4)])


def along(block, distance):
    size = lax.axis_size("replica")
    return lax.ppermute(block, "replica", [(i, i ^ distance) for i in range(size)])


def tie(*values):
    return lax.optimization_barrier(values)


def gather_direct(own):
    return [own] + [across(own, d) for d in (1, 2, 3)]


def add_low(*terms):
    total = terms[0].astype(F32)
    for term in terms[1:]:
        total = total + term.astype(F32)
    return total.astype(BF16)


def reduce_steps(keep, give, quick):
    (got,) = yield [swap(give)]
    total = add_low(keep, got)
    got = yield [across(total[d], d) for d in (1, 2, 3)]
    owned = add_low(total[0], *got)
    size = lax.axis_size("replica")
    if size != 4:
        return lax.psum(owned, "replica")
    if quick:
        for d in (1, 2):
            (got,) = yield [along(owned, d)]
            owned = add_low(owned, got)
        return owned
    at = lax.axis_index("replica")
    quarters = owned.reshape(4, -1, 512)

    def pick(d):
        return lax.dynamic_index_in_dim(quarters, at ^ d, 0, keepdims=False)

    got = yield [along(pick(d), d) for d in (1, 2, 3)]
    total = add_low(pick(0), *got)
    got = yield [along(total, d) for d in (1, 2, 3)]
    held = jnp.stack([total] + list(got))
    return held[jnp.bitwise_xor(jnp.arange(4), at)].reshape(owned.shape)


def sum_steps(block):
    size = lax.axis_size("replica")
    moves = [swap, lambda b: across(b, 1), lambda b: across(b, 2)]
    whole_bits = size & (size - 1) == 0
    if whole_bits:
        moves += [lambda b, d=1 << n: along(b, d) for n in range(size.bit_length() - 1)]
    for move in moves:
        (got,) = yield [move(block)]
        block = block + got
    return block if whole_bits else lax.psum(block, "replica")


class Flow:
    def __init__(self, steps):
        self.steps = steps
        self.sent = next(steps)
        self.total = None

    def take(self, sent):
        if self.total is None:
            try:
                self.sent = self.steps.send(list(sent))
            except StopIteration as end:
                self.total, self.sent = end.value, []


def boundary_of(values, flows):
    values, sent = tie(values, [flow.sent for flow in flows])
    for flow, block in zip(flows, sent):
        flow.take(block)
    return values


def body(
    boundary,
    norm_gains,
    biases,
    up_bias,
    offset_table,
    attention_in,
    attention_out,
    up_weight,
    down_weight,
    offset_index,
    regions,
    micro_counts,
):
    core = lax.axis_index("section")
    first = core == 0
    me = lax.axis_index("shard")
    mb_count, per_device = boundary.shape[1], boundary.shape[2]
    slots = mb_count * per_device
    share = (slots + 1) // 2

    present = (jnp.arange(per_device)[None] < micro_counts[:, None]).reshape(slots)
    rank = jnp.cumsum(present.astype(jnp.int32)) - 1
    owner = jnp.bitwise_and(rank, 1)
    place = jnp.right_shift(rank, 1)

    def slots_of(whose):
        hit = present & (owner == whose)
        hit = hit[None] & (place[None] == jnp.arange(share)[:, None])
        return jnp.sum(jnp.where(hit, jnp.arange(slots)[None], 0), 1)

    total_images = jnp.sum(present.astype(jnp.int32))
    own_count = jnp.right_shift(total_images + 1 - core, 1)
    info = jnp.stack([own_count, core, me]).astype(jnp.int32)

    flat = jnp.concatenate(
        [
            norm_gains[0].reshape(-1),
            biases[0].reshape(-1),
            up_bias[0].reshape(-1),
            offset_table[0].reshape(-1),
        ]
    )
    flat = jnp.pad(flat, (0, -flat.shape[0] % 1024)).reshape(-1, 128)

    def columns(weight):
        rows, cols = weight.shape
        return weight.reshape(2, rows // 2, cols // 512, 512).transpose(0, 2, 1, 3).reshape(2, -1, 512)

    attn_own = attention_in[0].reshape(128, 3, 512).transpose(1, 0, 2).reshape(384, 512)
    attn_own, up_weight, down_weight, attention_out, flat = tie(
        attn_own, up_weight, down_weight, attention_out, flat
    )
    attn_mine = jnp.stack([attn_own] + [across(attn_own, d) for d in (1, 2, 3)])
    attn_pieces = (attn_mine, swap(attn_mine))
    parts = jnp.concatenate(
        [
            columns(up_weight[0]),
            down_weight[0].reshape(2, 256, 512),
            attention_out[0].reshape(2, 64, 512),
        ],
        1,
    )
    keep, got = jnp.where(first, parts[0], parts[1]), swap(jnp.where(first, parts[1], parts[0]))
    mlp_own = [jnp.where(core == layer, keep, got) for layer in range(2)]
    mlp_first, boundary, _ = tie(mlp_own[0], boundary, attn_mine)
    mlp_mine = gather_direct(mlp_first)

    framed = boundary.reshape(slots, TOKENS, 512)
    framed = jnp.pad(framed, ((0, 0), (0, FRAME - TOKENS), (0, 0)))
    kept = framed[slots_of(core)]
    other = swap(framed[slots_of(1 - core)])
    images = jnp.where(first, kept, other)
    cotangents = jnp.where(first, other, kept)

    small = jnp.stack([flat] + [across(flat, d) for d in (1, 2, 3)])
    small = small[jnp.bitwise_xor(jnp.arange(4), me)]
    small_other = swap(small)
    small = jnp.stack([jnp.where(first, small, small_other), jnp.where(first, small_other, small)])
    small = small.reshape(2, 4, -1).astype(F32)
    rel = offset_table.shape[1]
    gains = small[:, :, 0:256].reshape(2, 4, 2, 128).transpose(0, 2, 1, 3).reshape(2, 2, 512)
    shifts = small[:, :, 256:1024].reshape(2, 4, 6, 128).transpose(0, 2, 1, 3).reshape(2, 6, 512)
    vecs = jnp.concatenate([gains, shifts], 1)
    lifts = small[:, :, 1024:1536].reshape(2, 1, 2048)
    tables = small[:, :, 1536 : 1536 + 4 * rel].reshape(2, 4, rel, 4).transpose(0, 2, 1, 3).reshape(2, rel, HEADS)

    spare = SLOT - LEN
    pairs = jnp.pad(offset_index.T, ((0, spare), (0, spare))).reshape(-1)
    onehot = (pairs[None, :] == jnp.arange(rel)[:, None]).astype(BF16)
    heads_first = tables.transpose(0, 2, 1).reshape(2 * HEADS, rel).astype(BF16)
    offsets = jnp.dot(heads_first, onehot, preferred_element_type=F32)
    offsets = offsets.reshape(2, GROUPS, QUAD, SLOT, SLOT).transpose(0, 1, 3, 2, 4)
    offsets = offsets.reshape(2, GROUPS, SLOT, WIDE)
    bias = jnp.where(jnp.arange(SLOT)[:, None] < LEN, offsets * LOG2E, -1e30)
    split = regions.reshape(2, WIN, 2, WIN).transpose(0, 2, 1, 3).reshape(WINS, LEN)
    split = jnp.pad(split, ((0, 0), (0, spare)))
    apart = jnp.where(split[:, :, None] == jnp.tile(split, (1, QUAD))[:, None, :], 0.0, -100.0 * LOG2E)
    apart = apart.astype(F32)

    cut = [jnp.asarray(window_place(shift), BF16) for shift in (0, SHIFT)]
    x, saved = images, []
    for layer in range(2):
        vec = vecs[layer]
        qkv, p, att = attn_forward(
            layer, info, attn_pieces, x, cut[layer], cut[layer].T, vec, bias[layer], apart
        )
        if layer == 0:
            att, mlp_mine, mlp_second = tie(att, mlp_mine, mlp_own[1])
            mlp_pieces = [mlp_mine + [swap(jnp.stack(mlp_mine))]]
            mlp_mine = gather_direct(mlp_second)
        out, mid, act, slope = mlp_forward(info, mlp_pieces[layer], x, att, vec, lifts[layer])
        if layer == 0:
            out, mlp_mine = tie(out, mlp_mine)
            mlp_pieces.append(mlp_mine + [swap(jnp.stack(mlp_mine))])
        saved.append((x, qkv, p, att, mid, act, slope))
        x = out
    output, g = x, cotangents
    small_sums = [None, None]

    def backward_mlp(layer, g):
        x, qkv, p, att, mid, act, slope = saved[layer]
        return mlp_backward(info, mlp_pieces[layer], g, att, mid, act, slope, vecs[layer])

    def backward_attn(layer, g_mid, g_att):
        x, qkv, p, *_ = saved[layer]
        return attn_backward(
            layer,
            info,
            attn_pieces,
            g_mid,
            g_att,
            x,
            qkv,
            p,
            cut[layer],
            cut[layer].T,
            vecs[layer],
        )

    def small_of(vec, up, table):
        table = table.reshape(GROUPS, SLOT, QUAD, SLOT).transpose(0, 2, 1, 3)
        table = table.reshape(HEADS, SLOT * SLOT)
        table = lax.dot_general(
            table, onehot.astype(F32), (((1,), (1,)), ((), ())), precision=lax.Precision.HIGHEST
        )
        return jnp.concatenate([vec.reshape(-1), up.reshape(-1), table.reshape(-1)])

    g_mid, g_att, *sums, mlp_vec, up_sums = backward_mlp(1, g)
    second_mlp = Flow(reduce_steps(*sums, False))
    g_mid, g_att = boundary_of((g_mid, g_att), [second_mlp])
    g, *sums, attn_vec, table = backward_attn(1, g_mid, g_att)
    second_small = (mlp_vec + attn_vec, up_sums, table)
    g, sums = boundary_of((g, sums), [second_mlp])
    second_attn = Flow(reduce_steps(*sums, True))
    g_mid, g_att, *sums, mlp_vec, up_sums = backward_mlp(0, g)
    g_mid, g_att, sums = boundary_of((g_mid, g_att, sums), [second_mlp, second_attn])
    first_mlp = Flow(reduce_steps(*sums, False))
    second_small = small_of(*second_small)
    g_mid, g_att, second_small = boundary_of((g_mid, g_att, second_small), [first_mlp])
    g, *sums, attn_vec, table = backward_attn(0, g_mid, g_att)
    g, sums = boundary_of((g, sums), [second_mlp, second_attn, first_mlp])
    first_attn = Flow(reduce_steps(*sums, True))
    g_image = g
    hold = jnp.where(first, g_image, output)
    back = swap(jnp.where(first, output, g_image))
    small = jnp.stack([small_of(mlp_vec + attn_vec, up_sums, table), second_small])
    width = small.shape[1]
    small = jnp.pad(small, ((0, 0), (0, -width % 1024))).reshape(-1, 128)
    small_flow = Flow(sum_steps(small))
    hold, back = boundary_of((hold, back), [first_attn, small_flow])

    every = jnp.concatenate([hold, back], 0)
    source = jnp.clip(jnp.where(owner == core, 0, share) + place, 0, 2 * share - 1)
    chosen = every[source][:, :TOKENS]
    chosen = jnp.where(present[:, None, None], chosen, jnp.zeros((), BF16))
    results = chosen.reshape(1, mb_count, per_device, SIDE, SIDE, 512)
    results = boundary_of(results, [first_attn, small_flow])
    flows = [first_attn, small_flow, second_attn, first_mlp, second_mlp]
    while any(flow.total is None for flow in flows):
        for flow in flows:
            flow.take(flow.sent)
    big = [
        jnp.concatenate([first_attn.total, first_mlp.total], 0),
        jnp.concatenate([second_attn.total, second_mlp.total], 0),
    ]

    hold = jnp.where(first, big[0], big[1])
    back = swap(jnp.where(first, big[1], big[0]))
    both = jnp.stack([jnp.where(first, hold, back), jnp.where(first, back, hold)]).astype(F32)
    grad_in = both[:, 0:192].reshape(2, 3, 64, 512).transpose(0, 2, 1, 3).reshape(128, 1536)
    grad_up = both[:, 192:448].reshape(2, 4, 64, 512).transpose(0, 2, 1, 3).reshape(128, 2048)
    grad_down = both[:, 448:704].reshape(512, 512)
    grad_out = both[:, 704:768].reshape(128, 512)

    bundle = small_flow.total.reshape(2, -1)[:, :width]
    bundle = lax.dynamic_index_in_dim(bundle, core, 0, keepdims=False)
    vec = lax.dynamic_slice_in_dim(bundle[:4096].reshape(8, 512), me * 128, 128, 1)
    grad_lift = lax.dynamic_slice_in_dim(bundle[4096:6144], me * 512, 512, 0)
    grad_table = lax.dynamic_slice_in_dim(bundle[6144:].reshape(HEADS, rel), me * 4, 4, 0).T

    return (
        results,
        vec[None, 0:2],
        vec[None, 2:8],
        grad_lift[None],
        grad_table[None],
        grad_in[None],
        grad_out[None],
        grad_up[None],
        grad_down[None],
    )


def solution(mesh):
    placed = (
        P("section", None, ("shard", "replica"), None, None, None),
        P("section", None, "shard"),
        P("section", None, "shard"),
        P("section", "shard"),
        P("section", None, "shard"),
        P("section", "shard", None),
        P("section", "shard", None),
        P("section", "shard", None),
        P("section", "shard", None),
        P(),
        P(),
        P(),
    )
    return jax.shard_map(
        body,
        mesh=mesh,
        in_specs=placed,
        out_specs=(placed[0],) + placed[1:9],
        check_vma=False,
    )
```

```python
import functools

import jax
import jax.numpy as jnp
import numpy as np
from jax import lax
from jax.experimental import pallas as pl
from jax.experimental.pallas import tpu as pltpu
from jax.sharding import PartitionSpec as P

WIN = 7
SIDE = 14
SHIFT = 3
LEN = WIN * WIN
WINS = 4
SLOT = 64
ROWS = WINS * SLOT
TOKENS = SIDE * SIDE
FRAME = 208
HEADS = 16
QUAD = 4
GROUPS = HEADS // QUAD
WIDE = QUAD * SLOT
LOG2E = 1.4426950408889634
F32 = jnp.float32
BF16 = jnp.bfloat16


def window_place(shift):
    place = np.zeros((ROWS, FRAME), np.float32)
    for window in range(WINS):
        for token in range(LEN):
            line = ((window // 2) * WIN + token // WIN + shift) % SIDE
            column = ((window % 2) * WIN + token % WIN + shift) % SIDE
            place[window * SLOT + token, line * SIDE + column] = 1.0
    return place


def mm(a, b):
    return jnp.dot(a, b, preferred_element_type=F32)


def mm_nt(a, b):
    return lax.dot_general(a, b, (((1,), (1,)), ((), ())), preferred_element_type=F32)


def mm_tn(a, b):
    return lax.dot_general(a, b, (((0,), (0,)), ((), ())), preferred_element_type=F32)


def standard(v):
    centered = v - jnp.mean(v, -1, keepdims=True)
    spread = jnp.mean(centered * centered, -1, keepdims=True)
    inverse = lax.rsqrt(spread + 1e-05)
    return centered * inverse, inverse


def gelu_pair(h):
    density = jnp.exp(-0.5 * h * h)
    t = 1.0 / (1.0 + (0.3275911 * 0.7071067811865476) * jnp.abs(h))
    poly = t * (
        0.5 * 0.254829592
        + t
        * (
            0.5 * -0.284496736
            + t * (0.5 * 1.421413741 + t * (0.5 * -1.453152027 + t * (0.5 * 1.061405429)))
        )
    )
    tail = poly * density
    cdf = jnp.where(h < 0, tail, 1.0 - tail)
    return h * cdf, cdf + h * (density * 0.3989422804014327)


def head_mask(shape):
    rows = lax.broadcasted_iota(jnp.int32, shape, 0) // SLOT
    lanes = lax.broadcasted_iota(jnp.int32, shape, 1) // 32
    return rows == lanes


def spread_heads(block, mask):
    return jnp.where(mask, jnp.concatenate([block] * QUAD, 0), jnp.zeros((), block.dtype))


def join_heads(blocks):
    lane = lax.broadcasted_iota(jnp.int32, (SLOT, 128), 1) // 32
    out = blocks[:SLOT]
    for h in range(1, QUAD):
        out = jnp.where(lane == h, blocks[h * SLOT : (h + 1) * SLOT], out)
    return out


def attn_load(layer, info, pieces, w_in, sems, clear=()):
    mine, other = pieces[:4], pieces[4:]

    def copies(source):
        pairs = []
        for at in range(4):
            row = pl.multiple_of(jnp.bitwise_xor(info[2], at) * 128, 128)
            for c in range(3):
                src = source[at].at[128 * c : 128 * c + 128]
                pairs.append((src, w_in.at[pl.ds(row, 128), 512 * c : 512 * c + 512]))
        return [pltpu.make_async_copy(*pair, sems.at[n]) for n, pair in enumerate(pairs)]

    @pl.when(pl.program_id(0) == 0)
    def _():
        @pl.when(info[1] == layer)
        def _():
            for c in copies(mine):
                c.start()

        @pl.when(info[1] != layer)
        def _():
            for c in copies(other):
                c.start()

        for total in clear:
            total[...] = jnp.zeros(total.shape, F32)
        for c in copies(mine):
            c.wait()


def mlp_copies(info, pieces, places, sems):
    w_out, w_up, w_down = places
    copies = []
    for half_at in range(2):
        half = jnp.bitwise_xor(info[1], half_at)
        for shard_at in range(4):
            shard = jnp.bitwise_xor(info[2], shard_at)
            piece = pieces[4 * half_at + shard_at]
            row = pl.multiple_of(shard * 128 + half * 64, 64)
            deep = pl.multiple_of(shard * 512 + half * 256, 256)
            pairs = [
                (piece.at[64 * c : 64 * c + 64], w_up.at[pl.ds(row, 64), 512 * c : 512 * c + 512])
                for c in range(4)
            ]
            pairs.append((piece.at[256:512], w_down.at[pl.ds(deep, 256), :]))
            pairs.append((piece.at[512:576], w_out.at[pl.ds(row, 64), :]))
            for src, dst in pairs:
                copies.append(pltpu.make_async_copy(src, dst, sems.at[len(copies)]))
    return copies


def group_lanes(g):
    return lambda part: slice(512 * part + 128 * g, 512 * part + 128 * g + 128)


BLOCKS = [
    (w, slice(w * SLOT, w * SLOT + SLOT), g, group_lanes(g))
    for w in range(WINS)
    for g in range(GROUPS)
]


def load_weights(copies, clear=()):
    @pl.when(pl.program_id(0) == 0)
    def _():
        for c in copies:
            c.start()
        for total in clear:
            total[...] = jnp.zeros(total.shape, F32)
        for c in copies:
            c.wait()


def attn_forward_kernel(layer, info, *refs):
    pieces, refs = refs[:8], refs[8:]
    x_ref, cut_ref, join_ref, vec_ref, bias_ref, apart_ref, *refs = refs
    qkv_ref, p_ref, att_ref, w_in, sems, att = refs
    attn_load(layer, info, pieces, w_in, sems)

    @pl.when(pl.program_id(0) < info[0])
    def _():
        xhat, _ = standard(x_ref[0].astype(F32))
        normed = (xhat * vec_ref[0:1] + vec_ref[2:3]).astype(BF16)
        normed = mm(cut_ref[...], normed).astype(BF16)
        for part in range(3):
            block = mm(normed, w_in[:, 512 * part : 512 * part + 512])
            if part != 1:
                row = 3 if part == 0 else 4
                block = block + vec_ref[row : row + 1]
            qkv_ref[0, :, 512 * part : 512 * part + 512] = block.astype(BF16)
        mask = head_mask((WIDE, 128))
        factor = 32**-0.5 * LOG2E

        scores, probs, outs = [], [], []
        for w, rows, g, lanes in BLOCKS:
            q = qkv_ref[0, rows, lanes(0)]
            bias = bias_ref[g] + apart_ref[w] if layer else bias_ref[g]
            scores.append(mm_nt(qkv_ref[0, rows, lanes(1)], spread_heads(q, mask)) * factor + bias)
        for s in scores:
            e = jnp.exp2(s - jnp.max(s, 0, keepdims=True))
            probs.append((e * (1.0 / jnp.sum(e, 0, keepdims=True))).astype(BF16))
        for p, (w, rows, g, lanes) in zip(probs, BLOCKS):
            outs.append(mm_tn(p, qkv_ref[0, rows, lanes(2)]))
        for p, out, (w, rows, g, lanes) in zip(probs, outs, BLOCKS):
            p_ref[0, w, g] = p
            att[rows, lanes(0)] = join_heads(out).astype(BF16)
        att_ref[0] = mm(join_ref[...], att[...]).astype(BF16)


def mlp_forward_kernel(info, *refs):
    pieces, refs = refs[:8], refs[8:]
    x_ref, att_ref, vec_ref, up_bias_ref, *refs = refs
    out_ref, mid_ref, act_ref, slope_ref, w_out, w_up, w_down, sems = refs
    load_weights(mlp_copies(info, pieces, (w_out, w_up, w_down), sems))

    @pl.when(pl.program_id(0) < info[0])
    def _():
        mid = x_ref[0].astype(F32) + (mm(att_ref[0], w_out[...]) + vec_ref[5:6])
        mid_ref[0] = mid
        xhat, _ = standard(mid)
        normed_two = (xhat * vec_ref[1:2] + vec_ref[6:7]).astype(BF16)
        cols = [slice(512 * c, 512 * c + 512) for c in range(4)]

        def lift(c):
            return mm(normed_two, w_up[:, cols[c]]) + up_bias_ref[:, cols[c]]

        hidden, active, down = lift(0), None, 0.0
        for c in range(4):
            after = lift(c + 1) if c < 3 else None
            before, (active, slope) = active, gelu_pair(hidden)
            active = active.astype(BF16)
            act_ref[0, :, cols[c]] = active
            slope_ref[0, :, cols[c]] = slope.astype(BF16)
            if c:
                down = down + mm(before, w_down[cols[c - 1], :])
            hidden = after
        down = down + mm(active, w_down[cols[3], :])
        out_ref[0] = (mid + (down + vec_ref[7:8])).astype(BF16)


def add_row(total, at, value):
    total[at : at + 1] += jnp.sum(value, 0, keepdims=True)


def norm_back(total, rows, g_normed, xhat, inverse, gain):
    add_row(total, rows[0], g_normed * xhat)
    add_row(total, rows[1], g_normed)
    u = g_normed * gain
    lean = jnp.mean(u * xhat, -1, keepdims=True)
    return (u - jnp.mean(u, -1, keepdims=True) - xhat * lean) * inverse


def mlp_backward_kernel(info, *refs):
    pieces, refs = refs[:8], refs[8:]
    g_ref, att_ref, mid_ref, act_ref, slope_ref, vec_ref, *refs = refs
    g_mid_ref, g_att_ref, keep_ref, give_ref, vec_out, up_out, *refs = refs
    w_out, w_up, w_down, sems, d_out, d_up, d_down = refs
    load_weights(
        mlp_copies(info, pieces, (w_out, w_up, w_down), sems),
        (d_out, d_up, d_down, vec_out, up_out),
    )

    @pl.when(pl.program_id(0) < info[0])
    def _():
        g = g_ref[0]
        add_row(vec_out, 7, g.astype(F32))
        xhat, inverse = standard(mid_ref[0])
        normed_two = (xhat * vec_ref[1:2] + vec_ref[6:7]).astype(BF16)
        cols = [slice(512 * c, 512 * c + 512) for c in range(4)]
        g_hidden = []
        for c in cols:
            part = (mm_nt(g, w_down[c, :]) * slope_ref[0, :, c].astype(F32)).astype(BF16)
            up_out[:, c] += jnp.sum(part.astype(F32), 0, keepdims=True)
            g_hidden.append(part)
        g_normed = sum(mm_nt(part, w_up[:, c]) for part, c in zip(g_hidden, cols))
        for part, c in zip(g_hidden, cols):
            d_down[:, c] += mm_tn(g, act_ref[0, :, c])
            d_up[:, c] += mm_tn(normed_two, part)
        g_mid = g.astype(F32) + norm_back(vec_out, (1, 6), g_normed, xhat, inverse, vec_ref[1:2])
        g_mid_ref[0] = g_mid
        g_update = g_mid.astype(BF16)
        add_row(vec_out, 5, g_update.astype(F32))
        d_out[...] += mm_tn(att_ref[0], g_update)
        g_att_ref[0] = mm_nt(g_update, w_out[...]).astype(BF16)

    @pl.when(pl.program_id(0) == pl.num_programs(0) - 1)
    def _():
        for out_ref, half in ((keep_ref, info[1]), (give_ref, 1 - info[1])):
            for shard in range(4):
                at = jnp.bitwise_xor(info[2], shard)
                rows = pl.ds(pl.multiple_of(128 * shard + 64 * half, 64), 64)
                for c in range(4):
                    out_ref[at, 64 * c : 64 * c + 64, :] = d_up[
                        rows, 512 * c : 512 * c + 512
                    ].astype(BF16)
                deep = pl.ds(pl.multiple_of(512 * shard + 256 * half, 256), 256)
                out_ref[at, 256:512, :] = d_down[:, deep].T.astype(BF16)
                out_ref[at, 512:576, :] = d_out[rows, :].astype(BF16)


def attn_backward_kernel(layer, info, *refs):
    pieces, refs = refs[:8], refs[8:]
    g_mid_ref, g_att_ref, x_ref, qkv_ref, p_ref, cut_ref, join_ref, vec_ref, *refs = refs
    gx_ref, keep_ref, give_ref, vec_out, table_out, *refs = refs
    w_in, sems, d_in, g_att, gqkv = refs
    attn_load(layer, info, pieces, w_in, sems, (d_in, vec_out, table_out))

    @pl.when(pl.program_id(0) < info[0])
    def _():
        g_att[...] = mm(cut_ref[...], g_att_ref[0]).astype(BF16)
        mask = head_mask((WIDE, 128))

        at = range(len(BLOCKS))
        q, k, v = [[qkv_ref[0, rows, lanes(n)] for _, rows, _, lanes in BLOCKS] for n in range(3)]
        p = [p_ref[0, w, h] for w, _, h, _ in BLOCKS]
        g_out = [spread_heads(g_att[rows, lanes(0)], mask) for _, rows, _, lanes in BLOCKS]
        g_p = [mm_nt(v[n], g_out[n]) for n in at]
        g_v = [mm(p[n], g_out[n]) for n in at]
        g_s = []
        for n in at:
            soft = p[n].astype(F32)
            part = soft * g_p[n]
            g_s.append((part - soft * jnp.sum(part, 0, keepdims=True)).astype(BF16))
        g_k = [mm(g_s[n], spread_heads(q[n], mask)) for n in at]
        g_q = [mm_tn(g_s[n], k[n]) for n in at]
        for n, (_, rows, _, lanes) in enumerate(BLOCKS):
            gqkv[rows, lanes(0)] = (join_heads(g_q[n]) * 32**-0.5).astype(BF16)
            gqkv[rows, lanes(1)] = (g_k[n] * 32**-0.5).astype(BF16)
            gqkv[rows, lanes(2)] = g_v[n].astype(BF16)
        for h in range(GROUPS):
            table_out[h] += sum(g_s[n].astype(F32) for n in at if BLOCKS[n][2] == h)
        xhat, inverse = standard(x_ref[0].astype(F32))
        normed = (xhat * vec_ref[0:1] + vec_ref[2:3]).astype(BF16)
        g_normed = None
        for part in range(3):
            cols = slice(512 * part, 512 * part + 512)
            block = mm(join_ref[...], gqkv[:, cols]).astype(BF16)
            d_in[:, cols] += mm_tn(normed, block)
            if part != 1:
                add_row(vec_out, 3 if part == 0 else 4, block.astype(F32))
            term = mm_nt(block, w_in[:, cols])
            g_normed = term if g_normed is None else g_normed + term
        back = norm_back(vec_out, (0, 2), g_normed, xhat, inverse, vec_ref[0:1])
        gx_ref[0] = (g_mid_ref[0] + back).astype(BF16)

    @pl.when(pl.program_id(0) == pl.num_programs(0) - 1)
    def _():
        for out_ref, half in ((keep_ref, info[1]), (give_ref, 1 - info[1])):
            for shard in range(4):
                at = jnp.bitwise_xor(info[2], shard)
                rows = pl.ds(pl.multiple_of(128 * shard + 64 * half, 64), 64)
                for c in range(3):
                    out_ref[at, 64 * c : 64 * c + 64, :] = d_in[
                        rows, 512 * c : 512 * c + 512
                    ].astype(BF16)


def whole(shape):
    return pl.BlockSpec(shape, lambda i, info: (0,) * len(shape))


def each(shape):
    return pl.BlockSpec(
        (1,) + shape,
        lambda i, info: (jnp.maximum(jnp.minimum(i, info[0] - 1), 0),) + (0,) * len(shape),
    )


X = ((FRAME, 512), BF16)
QKV = ((ROWS, 1536), BF16)
PROB = ((WINS, GROUPS, SLOT, WIDE), BF16)
MID = ((FRAME, 512), F32)
WIDE_X = ((FRAME, 2048), BF16)
VEC = ((8, 512), F32)
ATTN_WEIGHTS = [pltpu.VMEM((512, 1536), BF16), pltpu.SemaphoreType.DMA((12,))]
MLP_WEIGHTS = [
    pltpu.VMEM((512, 512), BF16),
    pltpu.VMEM((512, 2048), BF16),
    pltpu.VMEM((2048, 512), BF16),
    pltpu.SemaphoreType.DMA((48,)),
]


def run(kernel, info, pieces, by_image, shared, outs, shared_outs, scratch, micros):
    count = by_image[0].shape[0]
    return pl.pallas_call(
        kernel,
        grid_spec=pltpu.PrefetchScalarGridSpec(
            num_scalar_prefetch=1,
            grid=(count,),
            in_specs=[pl.BlockSpec(memory_space=pl.ANY)] * len(pieces)
            + [each(a.shape[1:]) for a in by_image]
            + [whole(a.shape) for a in shared],
            out_specs=[each(shape) for shape, _ in outs]
            + [whole(shape) for shape, _ in shared_outs],
            scratch_shapes=scratch,
        ),
        out_shape=[jax.ShapeDtypeStruct((count,) + shape, kind) for shape, kind in outs]
        + [jax.ShapeDtypeStruct(shape, kind) for shape, kind in shared_outs],
        compiler_params=pltpu.CompilerParams(vmem_limit_bytes=56 * 1024 * 1024),
        cost_estimate=pl.CostEstimate(
            flops=int(micros * 1e9), bytes_accessed=int(micros * 1e6), transcendentals=0
        ),
    )(info, *pieces, *by_image, *shared)


def attn_forward(layer, info, pieces, x, cut, join, vec, bias, apart):
    return run(
        functools.partial(attn_forward_kernel, layer),
        info,
        pieces,
        [x],
        [cut, join, vec, bias, apart],
        [QKV, PROB, X],
        [],
        ATTN_WEIGHTS + [pltpu.VMEM((ROWS, 512), BF16)],
        20,
    )


def mlp_forward(info, pieces, x, att, vec, up_bias):
    return run(
        mlp_forward_kernel,
        info,
        pieces,
        [x, att],
        [vec, up_bias],
        [X, MID, WIDE_X, WIDE_X],
        [],
        MLP_WEIGHTS,
        20,
    )


def mlp_backward(info, pieces, g, att, mid, act, slope, vec):
    return run(
        mlp_backward_kernel,
        info,
        pieces,
        [g, att, mid, act, slope],
        [vec],
        [MID, X],
        [((4, 576, 512), BF16)] * 2 + [VEC, ((1, 2048), F32)],
        MLP_WEIGHTS
        + [pltpu.VMEM((512, 512), F32), pltpu.VMEM((512, 2048), F32), pltpu.VMEM((512, 2048), F32)],
        30,
    )


def attn_backward(layer, info, pieces, g_mid, g_att, x, qkv, p, cut, join, vec):
    return run(
        functools.partial(attn_backward_kernel, layer),
        info,
        pieces,
        [g_mid, g_att, x, qkv, p],
        [cut, join, vec],
        [X],
        [((4, 192, 512), BF16)] * 2 + [VEC, ((GROUPS, SLOT, WIDE), F32)],
        ATTN_WEIGHTS
        + [
            pltpu.VMEM((512, 1536), F32),
            pltpu.VMEM((ROWS, 512), BF16),
            pltpu.VMEM((ROWS, 1536), BF16),
        ],
        30,
    )


def swap(block):
    return lax.ppermute(block, "section", [(0, 1), (1, 0)])


def across(block, distance):
    return lax.ppermute(block, "shard", [(i, i ^ distance) for i in range(4)])


def along(block, distance):
    size = lax.axis_size("replica")
    return lax.ppermute(block, "replica", [(i, i ^ distance) for i in range(size)])


def tie(*values):
    return lax.optimization_barrier(values)


def by_distance(stack, at):
    for bit in (1, 2):
        other = jnp.stack([stack[d ^ bit] for d in range(4)])
        stack = jnp.where(at & bit != 0, other, stack)
    return stack


def gather_direct(own):
    return [own] + [across(own, d) for d in (1, 2, 3)]


def with_other(pieces):
    return pieces + [swap(piece) for piece in pieces]


def add_low(*terms):
    total = terms[0].astype(F32)
    for term in terms[1:]:
        total = total + term.astype(F32)
    return total.astype(BF16)


def reduce_steps(keep, give, quick):
    (got,) = yield [swap(give)]
    total = add_low(keep, got)
    got = yield [across(total[d], d) for d in (1, 2, 3)]
    owned = add_low(total[0], *got)
    size = lax.axis_size("replica")
    if size != 4:
        return lax.psum(owned, "replica")
    if quick:
        for d in (1, 2):
            (got,) = yield [along(owned, d)]
            owned = add_low(owned, got)
        return owned
    at = lax.axis_index("replica")
    quarters = owned.reshape(4, -1, 512)

    def pick(d):
        return lax.dynamic_index_in_dim(quarters, at ^ d, 0, keepdims=False)

    got = yield [along(pick(d), d) for d in (1, 2, 3)]
    total = add_low(pick(0), *got)
    got = yield [along(total, d) for d in (1, 2, 3)]
    held = jnp.stack([total] + list(got))
    return by_distance(held, at).reshape(owned.shape)


def sum_steps(block):
    (got,) = yield [swap(block)]
    block = block + got
    got = yield [across(block, d) for d in (1, 2, 3)]
    block = block + got[0] + got[1] + got[2]
    if lax.axis_size("replica") != 4:
        return lax.psum(block, "replica")
    got = yield [along(block, d) for d in (1, 2, 3)]
    return block + got[0] + got[1] + got[2]


class Flow:
    def __init__(self, steps):
        self.steps = steps
        self.sent = next(steps)
        self.total = None

    def take(self, sent):
        if self.total is None:
            try:
                self.sent = self.steps.send(list(sent))
            except StopIteration as end:
                self.total, self.sent = end.value, []


def boundary_of(values, flows):
    values, sent = tie(values, [flow.sent for flow in flows])
    for flow, block in zip(flows, sent):
        flow.take(block)
    return values


def body(
    boundary,
    norm_gains,
    biases,
    up_bias,
    offset_table,
    attention_in,
    attention_out,
    up_weight,
    down_weight,
    offset_index,
    regions,
    micro_counts,
):
    core = lax.axis_index("section")
    first = core == 0
    me = lax.axis_index("shard")
    mb_count, per_device = boundary.shape[1], boundary.shape[2]
    slots = mb_count * per_device
    share = (slots + 1) // 2

    present = (jnp.arange(per_device)[None] < micro_counts[:, None]).reshape(slots)
    rank = jnp.cumsum(present.astype(jnp.int32)) - 1
    owner = jnp.bitwise_and(rank, 1)
    place = jnp.right_shift(rank, 1)

    def slots_of(whose):
        hit = present & (owner == whose)
        hit = hit[None] & (place[None] == jnp.arange(share)[:, None])
        return jnp.sum(jnp.where(hit, jnp.arange(slots)[None], 0), 1)

    total_images = jnp.sum(present.astype(jnp.int32))
    own_count = jnp.right_shift(total_images + 1 - core, 1)
    info = jnp.stack([own_count, core, me]).astype(jnp.int32)

    flat = jnp.concatenate(
        [
            norm_gains[0].reshape(-1),
            biases[0].reshape(-1),
            up_bias[0].reshape(-1),
            offset_table[0].reshape(-1),
        ]
    )
    flat = jnp.pad(flat, (0, -flat.shape[0] % 1024)).reshape(-1, 128)

    def columns(weight):
        rows, cols = weight.shape
        return weight.reshape(2, rows // 2, cols // 512, 512).transpose(0, 2, 1, 3).reshape(2, -1, 512)

    attn_own = attention_in[0].reshape(128, 3, 512).transpose(1, 0, 2).reshape(384, 512)
    attn_own, up_weight, down_weight, attention_out, flat, boundary = tie(
        attn_own, up_weight, down_weight, attention_out, flat, boundary
    )
    attn_mine = gather_direct(attn_own)
    attn_pieces = with_other(attn_mine)
    parts = jnp.concatenate(
        [
            columns(up_weight[0]),
            down_weight[0].reshape(2, 256, 512),
            attention_out[0].reshape(2, 64, 512),
        ],
        1,
    )
    keep, got = jnp.where(first, parts[0], parts[1]), swap(jnp.where(first, parts[1], parts[0]))
    mlp_own = [jnp.where(core == layer, keep, got) for layer in range(2)]
    mlp_first, _ = tie(mlp_own[0], attn_mine[1])
    mlp_mine = gather_direct(mlp_first)

    framed = boundary.reshape(slots, TOKENS, 512)
    framed = jnp.pad(framed, ((0, 0), (0, FRAME - TOKENS), (0, 0)))
    kept = framed[slots_of(core)]
    other = swap(framed[slots_of(1 - core)])
    images = jnp.where(first, kept, other)
    cotangents = jnp.where(first, other, kept)

    small = by_distance(jnp.stack([flat] + [across(flat, d) for d in (1, 2, 3)]), me)
    small_other = swap(small)
    small = jnp.stack([jnp.where(first, small, small_other), jnp.where(first, small_other, small)])
    small = small.reshape(2, 4, -1).astype(F32)
    rel = offset_table.shape[1]
    gains = small[:, :, 0:256].reshape(2, 4, 2, 128).transpose(0, 2, 1, 3).reshape(2, 2, 512)
    shifts = small[:, :, 256:1024].reshape(2, 4, 6, 128).transpose(0, 2, 1, 3).reshape(2, 6, 512)
    vecs = jnp.concatenate([gains, shifts], 1)
    lifts = small[:, :, 1024:1536].reshape(2, 1, 2048)
    tables = small[:, :, 1536 : 1536 + 4 * rel].reshape(2, 4, rel, 4).transpose(0, 2, 1, 3).reshape(2, rel, HEADS)

    spare = SLOT - LEN
    pairs = jnp.pad(offset_index.T, ((0, spare), (0, spare))).reshape(-1)
    onehot = (pairs[None, :] == jnp.arange(rel)[:, None]).astype(BF16)
    heads_first = tables.transpose(0, 2, 1).reshape(2 * HEADS, rel).astype(BF16)
    offsets = jnp.dot(heads_first, onehot, preferred_element_type=F32)
    offsets = offsets.reshape(2, GROUPS, QUAD, SLOT, SLOT).transpose(0, 1, 3, 2, 4)
    offsets = offsets.reshape(2, GROUPS, SLOT, WIDE)
    bias = jnp.where(jnp.arange(SLOT)[:, None] < LEN, offsets * LOG2E, -1e30)
    split = regions.reshape(2, WIN, 2, WIN).transpose(0, 2, 1, 3).reshape(WINS, LEN)
    split = jnp.pad(split, ((0, 0), (0, spare)))
    apart = jnp.where(split[:, :, None] == jnp.tile(split, (1, QUAD))[:, None, :], 0.0, -100.0 * LOG2E)
    apart = apart.astype(F32)

    cut = [jnp.asarray(window_place(shift), BF16) for shift in (0, SHIFT)]
    x, saved = images, []
    for layer in range(2):
        vec = vecs[layer]
        qkv, p, att = attn_forward(
            layer, info, attn_pieces, x, cut[layer], cut[layer].T, vec, bias[layer], apart
        )
        if layer == 0:
            att, mlp_mine, mlp_second = tie(att, mlp_mine, mlp_own[1])
            mlp_pieces = [with_other(mlp_mine)]
            mlp_mine = gather_direct(mlp_second)
        out, mid, act, slope = mlp_forward(info, mlp_pieces[layer], x, att, vec, lifts[layer])
        if layer == 0:
            out, mlp_mine = tie(out, mlp_mine)
            mlp_pieces.append(with_other(mlp_mine))
        saved.append((x, qkv, p, att, mid, act, slope))
        x = out
    output, g = x, cotangents
    small_sums = [None, None]

    def backward_mlp(layer, g):
        x, qkv, p, att, mid, act, slope = saved[layer]
        return mlp_backward(info, mlp_pieces[layer], g, att, mid, act, slope, vecs[layer])

    def backward_attn(layer, g_mid, g_att):
        x, qkv, p, *_ = saved[layer]
        return attn_backward(
            layer,
            info,
            attn_pieces,
            g_mid,
            g_att,
            x,
            qkv,
            p,
            cut[layer],
            cut[layer].T,
            vecs[layer],
        )

    def small_of(vec, up, table):
        table = table.reshape(GROUPS, SLOT, QUAD, SLOT).transpose(0, 2, 1, 3)
        table = table.reshape(HEADS, SLOT * SLOT)
        table = lax.dot_general(
            table, onehot.astype(F32), (((1,), (1,)), ((), ())), precision=lax.Precision.HIGHEST
        )
        return jnp.concatenate([vec.reshape(-1), up.reshape(-1), table.reshape(-1)])

    g_mid, g_att, *sums, mlp_vec, up_sums = backward_mlp(1, g)
    second_mlp = Flow(reduce_steps(*sums, False))
    g_mid, g_att = boundary_of((g_mid, g_att), [second_mlp])
    g, *sums, attn_vec, table = backward_attn(1, g_mid, g_att)
    second_small = (mlp_vec + attn_vec, up_sums, table)
    g, sums = boundary_of((g, sums), [second_mlp])
    second_attn = Flow(reduce_steps(*sums, True))
    g = boundary_of(g, [second_attn])
    g_mid, g_att, *sums, mlp_vec, up_sums = backward_mlp(0, g)
    second_small = small_of(*second_small)
    g_mid, g_att, sums, second_small = boundary_of(
        (g_mid, g_att, sums, second_small), [second_mlp, second_attn]
    )
    first_mlp = Flow(reduce_steps(*sums, False))
    g_mid, g_att = boundary_of((g_mid, g_att), [first_mlp])
    g, *sums, attn_vec, table = backward_attn(0, g_mid, g_att)
    first_attn = Flow(reduce_steps(*sums, True))
    g = boundary_of(g, [second_mlp, second_attn, first_mlp])
    hold = jnp.where(first, g, output)
    back = swap(jnp.where(first, output, g))
    small = jnp.stack([small_of(mlp_vec + attn_vec, up_sums, table), second_small])
    width = small.shape[1]
    small = jnp.pad(small, ((0, 0), (0, -width % 1024))).reshape(-1, 128)
    back, small = boundary_of((back, small), [first_attn])
    small_flow = Flow(sum_steps(small))

    every = jnp.concatenate([hold, back], 0)
    source = jnp.clip(jnp.where(owner == core, 0, share) + place, 0, 2 * share - 1)
    chosen = every[source][:, :TOKENS]
    chosen = jnp.where(present[:, None, None], chosen, jnp.zeros((), BF16))
    results = chosen.reshape(1, mb_count, per_device, SIDE, SIDE, 512)
    results = boundary_of(results, [first_attn, small_flow, first_mlp, second_attn])
    flows = [first_attn, small_flow, second_attn, first_mlp, second_mlp]
    while any(flow.total is None for flow in flows[1:]):
        boundary_of((), flows)

    def exchanged(one, two):
        hold = jnp.where(first, one, two)
        back = swap(jnp.where(first, two, one))
        return jnp.stack([jnp.where(first, hold, back), jnp.where(first, back, hold)])

    mlp = exchanged(first_mlp.total, second_mlp.total)
    while first_attn.total is None:
        (mlp,) = boundary_of((mlp,), [first_attn])
    mlp = mlp.astype(F32)
    attn = exchanged(first_attn.total, second_attn.total).astype(F32)
    grad_in = attn.reshape(2, 3, 64, 512).transpose(0, 2, 1, 3).reshape(128, 1536)
    grad_up = mlp[:, 0:256].reshape(2, 4, 64, 512).transpose(0, 2, 1, 3).reshape(128, 2048)
    grad_down = mlp[:, 256:512].reshape(512, 512)
    grad_out = mlp[:, 512:576].reshape(128, 512)

    bundle = small_flow.total.reshape(2, -1)[:, :width]
    bundle = lax.dynamic_index_in_dim(bundle, core, 0, keepdims=False)
    vec = lax.dynamic_slice_in_dim(bundle[:4096].reshape(8, 512), me * 128, 128, 1)
    grad_lift = lax.dynamic_slice_in_dim(bundle[4096:6144], me * 512, 512, 0)
    grad_table = lax.dynamic_slice_in_dim(bundle[6144:].reshape(HEADS, rel), me * 4, 4, 0).T

    return (
        results,
        vec[None, 0:2],
        vec[None, 2:8],
        grad_lift[None],
        grad_table[None],
        grad_in[None],
        grad_out[None],
        grad_up[None],
        grad_down[None],
    )


def solution(mesh):
    placed = (
        P("section", None, ("shard", "replica"), None, None, None),
        P("section", None, "shard"),
        P("section", None, "shard"),
        P("section", "shard"),
        P("section", None, "shard"),
        P("section", "shard", None),
        P("section", "shard", None),
        P("section", "shard", None),
        P("section", "shard", None),
        P(),
        P(),
        P(),
    )
    return jax.shard_map(
        body,
        mesh=mesh,
        in_specs=placed,
        out_specs=(placed[0],) + placed[1:9],
        check_vma=False,
    )
```

```python
import functools

import jax
import jax.numpy as jnp
import numpy as np
from jax import lax
from jax.experimental import pallas as pl
from jax.experimental.pallas import tpu as pltpu
from jax.sharding import PartitionSpec as P

WIN = 7
SIDE = 14
SHIFT = 3
LEN = WIN * WIN
WINS = 4
SLOT = 64
ROWS = WINS * SLOT
TOKENS = SIDE * SIDE
FRAME = 208
HEADS = 16
QUAD = 4
GROUPS = HEADS // QUAD
WIDE = QUAD * SLOT
LOG2E = 1.4426950408889634
F32 = jnp.float32
BF16 = jnp.bfloat16


def window_place(shift):
    place = np.zeros((ROWS, FRAME), np.float32)
    for window in range(WINS):
        for token in range(LEN):
            line = ((window // 2) * WIN + token // WIN + shift) % SIDE
            column = ((window % 2) * WIN + token % WIN + shift) % SIDE
            place[window * SLOT + token, line * SIDE + column] = 1.0
    return place


def mm(a, b):
    return jnp.dot(a, b, preferred_element_type=F32)


def mm_nt(a, b):
    return lax.dot_general(a, b, (((1,), (1,)), ((), ())), preferred_element_type=F32)


def mm_tn(a, b):
    return lax.dot_general(a, b, (((0,), (0,)), ((), ())), preferred_element_type=F32)


def standard(v):
    centered = v - jnp.mean(v, -1, keepdims=True)
    spread = jnp.mean(centered * centered, -1, keepdims=True)
    inverse = lax.rsqrt(spread + 1e-05)
    return centered * inverse, inverse


def gelu_pair(h):
    density = jnp.exp(-0.5 * h * h)
    t = 1.0 / (1.0 + (0.3275911 * 0.7071067811865476) * jnp.abs(h))
    poly = t * (
        0.5 * 0.254829592
        + t
        * (
            0.5 * -0.284496736
            + t * (0.5 * 1.421413741 + t * (0.5 * -1.453152027 + t * (0.5 * 1.061405429)))
        )
    )
    tail = poly * density
    cdf = jnp.where(h < 0, tail, 1.0 - tail)
    return h * cdf, cdf + h * (density * 0.3989422804014327)


def head_mask(shape):
    rows = lax.broadcasted_iota(jnp.int32, shape, 0) // SLOT
    lanes = lax.broadcasted_iota(jnp.int32, shape, 1) // 32
    return rows == lanes


def spread_heads(block, mask):
    return jnp.where(mask, jnp.concatenate([block] * QUAD, 0), jnp.zeros((), block.dtype))


def join_heads(blocks):
    lane = lax.broadcasted_iota(jnp.int32, (SLOT, 128), 1) // 32
    out = blocks[:SLOT]
    for h in range(1, QUAD):
        out = jnp.where(lane == h, blocks[h * SLOT : (h + 1) * SLOT], out)
    return out


def attn_load(layer, info, pieces, w_in, sems):
    mine, other = pieces[:4], pieces[4:]

    def copies(source):
        pairs = []
        for at in range(4):
            row = pl.multiple_of(jnp.bitwise_xor(info[2], at) * 128, 128)
            for c in range(3):
                src = source[at].at[128 * c : 128 * c + 128]
                pairs.append((src, w_in.at[pl.ds(row, 128), 512 * c : 512 * c + 512]))
        return [pltpu.make_async_copy(*pair, sems.at[n]) for n, pair in enumerate(pairs)]

    @pl.when(pl.program_id(0) == 0)
    def _():
        @pl.when(info[1] == layer)
        def _():
            for c in copies(mine):
                c.start()

        @pl.when(info[1] != layer)
        def _():
            for c in copies(other):
                c.start()

    return lambda: wait_first(copies(mine))


def mlp_copies(info, pieces, places, sems):
    w_out, w_up, w_down = places
    copies = []
    for half_at in range(2):
        half = jnp.bitwise_xor(info[1], half_at)
        for shard_at in range(4):
            shard = jnp.bitwise_xor(info[2], shard_at)
            piece = pieces[4 * half_at + shard_at]
            row = pl.multiple_of(shard * 128 + half * 64, 64)
            deep = pl.multiple_of(shard * 512 + half * 256, 256)
            pairs = [
                (piece.at[64 * c : 64 * c + 64], w_up.at[pl.ds(row, 64), 512 * c : 512 * c + 512])
                for c in range(4)
            ]
            pairs.append((piece.at[256:512], w_down.at[pl.ds(deep, 256), :]))
            pairs.append((piece.at[512:576], w_out.at[pl.ds(row, 64), :]))
            for src, dst in pairs:
                copies.append(pltpu.make_async_copy(src, dst, sems.at[len(copies)]))
    return copies


def group_lanes(g):
    return lambda part: slice(512 * part + 128 * g, 512 * part + 128 * g + 128)


BLOCKS = [
    (w, slice(w * SLOT, w * SLOT + SLOT), g, group_lanes(g))
    for w in range(WINS)
    for g in range(GROUPS)
]


def start_first(copies):
    @pl.when(pl.program_id(0) == 0)
    def _():
        for c in copies:
            c.start()


def wait_first(copies):
    @pl.when(pl.program_id(0) == 0)
    def _():
        for c in copies:
            c.wait()


def clear_first(*totals):
    @pl.when(pl.program_id(0) == 0)
    def _():
        for total in totals:
            total[...] = jnp.zeros(total.shape, F32)


def accumulate(total, at, value):
    total[at] = jnp.where(pl.program_id(0) == 0, 0.0, total[at]) + value


def pick(info, section, refs):
    if len(refs) == 1:
        return refs[0][0]
    own, other = refs
    return jnp.where(info[1] == section, own[0], other[0])


def attn_forward_kernel(layer, info, *refs):
    pieces, refs = refs[:8], refs[8:]
    count = 1 if layer else 2
    x_refs, refs = refs[:count], refs[count:]
    cut_ref, join_ref, vec_ref, bias_ref, apart_ref, *refs = refs
    qkv_ref, p_ref, att_ref, *x_out, w_in, sems, att = refs
    arrived = attn_load(layer, info, pieces, w_in, sems)

    @pl.when(pl.program_id(0) < info[0])
    def _():
        x = pick(info, 0, x_refs)
        for ref in x_out:
            ref[0] = x
        xhat, _ = standard(x.astype(F32))
        normed = (xhat * vec_ref[0:1] + vec_ref[2:3]).astype(BF16)
        normed = mm(cut_ref[...], normed).astype(BF16)
        arrived()
        for part in range(3):
            block = mm(normed, w_in[:, 512 * part : 512 * part + 512])
            if part != 1:
                row = 3 if part == 0 else 4
                block = block + vec_ref[row : row + 1]
            qkv_ref[0, :, 512 * part : 512 * part + 512] = block.astype(BF16)
        mask = head_mask((WIDE, 128))
        factor = 32**-0.5 * LOG2E

        scores, probs, outs = [], [], []
        for w, rows, g, lanes in BLOCKS:
            q = qkv_ref[0, rows, lanes(0)]
            bias = bias_ref[g] + apart_ref[w] if layer else bias_ref[g]
            scores.append(mm_nt(qkv_ref[0, rows, lanes(1)], spread_heads(q, mask)) * factor + bias)
        for s in scores:
            e = jnp.exp2(s - jnp.max(s, 0, keepdims=True))
            probs.append((e * (1.0 / jnp.sum(e, 0, keepdims=True))).astype(BF16))
        for p, (w, rows, g, lanes) in zip(probs, BLOCKS):
            outs.append(mm_tn(p, qkv_ref[0, rows, lanes(2)]))
        for p, out, (w, rows, g, lanes) in zip(probs, outs, BLOCKS):
            p_ref[0, w, g] = p
            att[rows, lanes(0)] = join_heads(out).astype(BF16)
        att_ref[0] = mm(join_ref[...], att[...]).astype(BF16)


def mlp_forward_kernel(info, *refs):
    pieces, refs = refs[:8], refs[8:]
    x_ref, att_ref, vec_ref, up_bias_ref, *refs = refs
    out_ref, mid_ref, act_ref, slope_ref, w_out, w_up, w_down, sems = refs
    copies = mlp_copies(info, pieces, (w_out, w_up, w_down), sems)
    start_first(copies)

    @pl.when(pl.program_id(0) < info[0])
    def _():
        wait_first(copies)
        mid = x_ref[0].astype(F32) + (mm(att_ref[0], w_out[...]) + vec_ref[5:6])
        mid_ref[0] = mid
        xhat, _ = standard(mid)
        normed_two = (xhat * vec_ref[1:2] + vec_ref[6:7]).astype(BF16)
        cols = [slice(512 * c, 512 * c + 512) for c in range(4)]

        def lift(c):
            return mm(normed_two, w_up[:, cols[c]]) + up_bias_ref[:, cols[c]]

        hidden, active, down = lift(0), None, 0.0
        for c in range(4):
            after = lift(c + 1) if c < 3 else None
            before, (active, slope) = active, gelu_pair(hidden)
            active = active.astype(BF16)
            act_ref[0, :, cols[c]] = active
            slope_ref[0, :, cols[c]] = slope.astype(BF16)
            if c:
                down = down + mm(before, w_down[cols[c - 1], :])
            hidden = after
        down = down + mm(active, w_down[cols[3], :])
        out_ref[0] = (mid + (down + vec_ref[7:8])).astype(BF16)


def add_row(total, at, value):
    total[at : at + 1] += jnp.sum(value, 0, keepdims=True)


def norm_back(total, rows, g_normed, xhat, inverse, gain):
    add_row(total, rows[0], g_normed * xhat)
    add_row(total, rows[1], g_normed)
    u = g_normed * gain
    lean = jnp.mean(u * xhat, -1, keepdims=True)
    return (u - jnp.mean(u, -1, keepdims=True) - xhat * lean) * inverse


def mlp_backward_kernel(layer, info, *refs):
    pieces, refs = refs[:8], refs[8:]
    count = 2 if layer else 1
    g_refs, refs = refs[:count], refs[count:]
    att_ref, mid_ref, act_ref, slope_ref, vec_ref, *refs = refs
    g_mid_ref, g_att_ref, keep_ref, give_ref, vec_out, up_out, *refs = refs
    w_out, w_up, w_down, sems, d_out, d_up, d_down = refs
    copies = mlp_copies(info, pieces, (w_out, w_up, w_down), sems)
    start_first(copies)
    clear_first(vec_out, up_out)

    @pl.when(pl.program_id(0) < info[0])
    def _():
        g = pick(info, 1, g_refs)
        cols = [slice(512 * c, 512 * c + 512) for c in range(4)]
        for c in cols:
            accumulate(d_down, (c, slice(None)), mm_tn(act_ref[0, :, c], g))
        add_row(vec_out, 7, g.astype(F32))
        xhat, inverse = standard(mid_ref[0])
        normed_two = (xhat * vec_ref[1:2] + vec_ref[6:7]).astype(BF16)
        wait_first(copies)
        g_hidden = []
        for c in cols:
            part = (mm_nt(g, w_down[c, :]) * slope_ref[0, :, c].astype(F32)).astype(BF16)
            up_out[:, c] += jnp.sum(part.astype(F32), 0, keepdims=True)
            g_hidden.append(part)
        g_normed = sum(mm_nt(part, w_up[:, c]) for part, c in zip(g_hidden, cols))
        for part, c in zip(g_hidden, cols):
            accumulate(d_up, (slice(None), c), mm_tn(normed_two, part))
        g_mid = g.astype(F32) + norm_back(vec_out, (1, 6), g_normed, xhat, inverse, vec_ref[1:2])
        g_mid_ref[0] = g_mid
        g_update = g_mid.astype(BF16)
        add_row(vec_out, 5, g_update.astype(F32))
        accumulate(d_out, Ellipsis, mm_tn(att_ref[0], g_update))
        g_att_ref[0] = mm_nt(g_update, w_out[...]).astype(BF16)

    @pl.when(pl.program_id(0) == pl.num_programs(0) - 1)
    def _():
        for out_ref, half in ((keep_ref, info[1]), (give_ref, 1 - info[1])):
            for shard in range(4):
                at = jnp.bitwise_xor(info[2], shard)
                rows = pl.ds(pl.multiple_of(128 * shard + 64 * half, 64), 64)
                for c in range(4):
                    out_ref[at, 64 * c : 64 * c + 64, :] = d_up[
                        rows, 512 * c : 512 * c + 512
                    ].astype(BF16)
                deep = pl.ds(pl.multiple_of(512 * shard + 256 * half, 256), 256)
                out_ref[at, 256:512, :] = d_down[deep, :].astype(BF16)
                out_ref[at, 512:576, :] = d_out[rows, :].astype(BF16)


def attn_backward_kernel(layer, info, *refs):
    pieces, refs = refs[:8], refs[8:]
    g_mid_ref, g_att_ref, x_ref, qkv_ref, p_ref, cut_ref, join_ref, vec_ref, *refs = refs
    gx_ref, keep_ref, give_ref, vec_out, table_out, *refs = refs
    w_in, sems, d_in, g_att, gqkv, table_sum = refs
    arrived = attn_load(layer, info, pieces, w_in, sems)
    clear_first(vec_out, table_sum)

    @pl.when(pl.program_id(0) < info[0])
    def _():
        g_att[...] = mm(cut_ref[...], g_att_ref[0]).astype(BF16)
        mask = head_mask((WIDE, 128))

        at = range(len(BLOCKS))
        q, k, v = [[qkv_ref[0, rows, lanes(n)] for _, rows, _, lanes in BLOCKS] for n in range(3)]
        p = [p_ref[0, w, h] for w, _, h, _ in BLOCKS]
        g_out = [spread_heads(g_att[rows, lanes(0)], mask) for _, rows, _, lanes in BLOCKS]
        g_p = [mm_nt(v[n], g_out[n]) for n in at]
        g_v = [mm(p[n], g_out[n]) for n in at]
        g_s = []
        for n in at:
            soft = p[n].astype(F32)
            part = soft * g_p[n]
            g_s.append((part - soft * jnp.sum(part, 0, keepdims=True)).astype(BF16))
        g_k = [mm(g_s[n], spread_heads(q[n], mask)) for n in at]
        g_q = [mm_tn(g_s[n], k[n]) for n in at]
        for n, (_, rows, _, lanes) in enumerate(BLOCKS):
            gqkv[rows, lanes(0)] = (join_heads(g_q[n]) * 32**-0.5).astype(BF16)
            gqkv[rows, lanes(1)] = (g_k[n] * 32**-0.5).astype(BF16)
            gqkv[rows, lanes(2)] = g_v[n].astype(BF16)
        for h in range(GROUPS):
            table_sum[h] += sum(g_s[n].astype(F32) for n in at if BLOCKS[n][2] == h)
        arrived()
        xhat, inverse = standard(x_ref[0].astype(F32))
        normed = (xhat * vec_ref[0:1] + vec_ref[2:3]).astype(BF16)
        g_normed = None
        for part in range(3):
            cols = slice(512 * part, 512 * part + 512)
            block = mm(join_ref[...], gqkv[:, cols]).astype(BF16)
            accumulate(d_in, (slice(None), cols), mm_tn(normed, block))
            if part != 1:
                add_row(vec_out, 3 if part == 0 else 4, block.astype(F32))
            term = mm_nt(block, w_in[:, cols])
            g_normed = term if g_normed is None else g_normed + term
        back = norm_back(vec_out, (0, 2), g_normed, xhat, inverse, vec_ref[0:1])
        gx_ref[0] = (g_mid_ref[0] + back).astype(BF16)

    @pl.when(pl.program_id(0) == pl.num_programs(0) - 1)
    def _():
        for h in range(HEADS):
            lanes = slice(h % QUAD * SLOT, h % QUAD * SLOT + SLOT)
            table_out[h] = table_sum[h // QUAD, :, lanes]
        for out_ref, half in ((keep_ref, info[1]), (give_ref, 1 - info[1])):
            for shard in range(4):
                at = jnp.bitwise_xor(info[2], shard)
                rows = pl.ds(pl.multiple_of(128 * shard + 64 * half, 64), 64)
                for c in range(3):
                    out_ref[at, 64 * c : 64 * c + 64, :] = d_in[
                        rows, 512 * c : 512 * c + 512
                    ].astype(BF16)


def whole(shape):
    return pl.BlockSpec(shape, lambda i, info: (0,) * len(shape))


def each(shape):
    return pl.BlockSpec(
        (1,) + shape,
        lambda i, info: (jnp.maximum(jnp.minimum(i, info[0] - 1), 0),) + (0,) * len(shape),
    )


X = ((FRAME, 512), BF16)
QKV = ((ROWS, 1536), BF16)
PROB = ((WINS, GROUPS, SLOT, WIDE), BF16)
MID = ((FRAME, 512), F32)
WIDE_X = ((FRAME, 2048), BF16)
VEC = ((8, 512), F32)
ATTN_WEIGHTS = [pltpu.VMEM((512, 1536), BF16), pltpu.SemaphoreType.DMA((12,))]
MLP_WEIGHTS = [
    pltpu.VMEM((512, 512), BF16),
    pltpu.VMEM((512, 2048), BF16),
    pltpu.VMEM((2048, 512), BF16),
    pltpu.SemaphoreType.DMA((48,)),
]


def by_slot(shape):
    def place(i, info):
        return (info[3 + jnp.maximum(jnp.minimum(i, info[0] - 1), 0)],) + (0,) * len(shape)

    return pl.BlockSpec((1,) + shape, place)


def run(kernel, info, pieces, slotted, by_image, shared, outs, shared_outs, scratch, micros, slot_outs=()):
    count = info.shape[0] - 3
    return pl.pallas_call(
        kernel,
        grid_spec=pltpu.PrefetchScalarGridSpec(
            num_scalar_prefetch=1,
            grid=(count,),
            in_specs=[pl.BlockSpec(memory_space=pl.ANY)] * len(pieces)
            + [by_slot(a.shape[1:]) for a in slotted]
            + [each(a.shape[1:]) for a in by_image]
            + [whole(a.shape) for a in shared],
            out_specs=[by_slot(shape[1:]) for shape, _ in slot_outs]
            + [each(shape) for shape, _ in outs]
            + [whole(shape) for shape, _ in shared_outs],
            scratch_shapes=scratch,
        ),
        out_shape=[jax.ShapeDtypeStruct(shape, kind) for shape, kind in slot_outs]
        + [jax.ShapeDtypeStruct((count,) + shape, kind) for shape, kind in outs]
        + [jax.ShapeDtypeStruct(shape, kind) for shape, kind in shared_outs],
        compiler_params=pltpu.CompilerParams(vmem_limit_bytes=56 * 1024 * 1024),
        cost_estimate=pl.CostEstimate(
            flops=int(micros * 1e9), bytes_accessed=int(micros * 1e6), transcendentals=0
        ),
    )(info, *pieces, *slotted, *by_image, *shared)


def attn_forward(layer, info, pieces, x, cut, join, vec, bias, apart):
    return run(
        functools.partial(attn_forward_kernel, layer),
        info,
        pieces,
        [] if layer else x,
        [x] if layer else [],
        [cut, join, vec, bias, apart],
        [QKV, PROB, X] + ([] if layer else [X]),
        [],
        ATTN_WEIGHTS + [pltpu.VMEM((ROWS, 512), BF16)],
        20,
    )


def mlp_forward(info, pieces, x, att, vec, up_bias, slots=None):
    return run(
        mlp_forward_kernel,
        info,
        pieces,
        [],
        [x, att],
        [vec, up_bias],
        ([] if slots else [X]) + [MID, WIDE_X, WIDE_X],
        [],
        MLP_WEIGHTS,
        20,
        [((slots,) + X[0], BF16)] if slots else [],
    )


def mlp_backward(layer, info, pieces, g, att, mid, act, slope, vec):
    return run(
        functools.partial(mlp_backward_kernel, layer),
        info,
        pieces,
        g if layer else [],
        ([] if layer else [g]) + [att, mid, act, slope],
        [vec],
        [MID, X],
        [((4, 576, 512), BF16)] * 2 + [VEC, ((1, 2048), F32)],
        MLP_WEIGHTS
        + [pltpu.VMEM((512, 512), F32), pltpu.VMEM((512, 2048), F32), pltpu.VMEM((2048, 512), F32)],
        30,
    )


def attn_backward(layer, info, pieces, g_mid, g_att, x, qkv, p, cut, join, vec, slots=None):
    return run(
        functools.partial(attn_backward_kernel, layer),
        info,
        pieces,
        [],
        [g_mid, g_att, x, qkv, p],
        [cut, join, vec],
        [] if slots else [X],
        [((4, 192, 512), BF16)] * 2 + [VEC, ((HEADS, SLOT, SLOT), F32)],
        ATTN_WEIGHTS
        + [
            pltpu.VMEM((512, 1536), F32),
            pltpu.VMEM((ROWS, 512), BF16),
            pltpu.VMEM((ROWS, 1536), BF16),
            pltpu.VMEM((GROUPS, SLOT, WIDE), F32),
        ],
        30,
        [((slots,) + X[0], BF16)] if slots else [],
    )


def swap(block):
    return lax.ppermute(block, "section", [(0, 1), (1, 0)])


def across(block, distance):
    return lax.ppermute(block, "shard", [(i, i ^ distance) for i in range(4)])


def along(block, distance):
    size = lax.axis_size("replica")
    return lax.ppermute(block, "replica", [(i, i ^ distance) for i in range(size)])


def tie(*values):
    return lax.optimization_barrier(values)


def by_distance(stack, at):
    for bit in (1, 2):
        other = jnp.stack([stack[d ^ bit] for d in range(4)])
        stack = jnp.where(at & bit != 0, other, stack)
    return stack


def gather_direct(own):
    return [own] + [across(own, d) for d in (1, 2, 3)]


def with_other(pieces):
    return pieces + [swap(piece) for piece in pieces]


def add_low(*terms):
    total = terms[0].astype(F32)
    for term in terms[1:]:
        total = total + term.astype(F32)
    return total.astype(BF16)


def reduce_steps(keep, give, quick):
    (got,) = yield [swap(give)]
    total = [add_low(keep[d], got[d]) for d in range(4)]
    got = yield [across(total[d], d) for d in (1, 2, 3)]
    owned = add_low(total[0], *got)
    size = lax.axis_size("replica")
    if size != 4:
        return lax.psum(owned, "replica")
    if quick:
        for d in quick:
            (got,) = yield [along(owned, d)]
            owned = add_low(owned, got)
        return owned
    at = lax.axis_index("replica")
    quarters = owned.reshape(4, -1, 512)

    def pick(d):
        return lax.dynamic_index_in_dim(quarters, at ^ d, 0, keepdims=False)

    got = yield [along(pick(d), d) for d in (1, 2, 3)]
    total = add_low(pick(0), *got)
    got = yield [along(total, d) for d in (1, 2, 3)]
    held = jnp.stack([total] + list(got))
    return by_distance(held, at).reshape(owned.shape)


def sum_steps(block):
    (got,) = yield [swap(block)]
    block = block + got
    got = yield [across(block, d) for d in (1, 2, 3)]
    block = block + got[0] + got[1] + got[2]
    if lax.axis_size("replica") != 4:
        return lax.psum(block, "replica")
    got = yield [along(block, d) for d in (1, 2, 3)]
    return block + got[0] + got[1] + got[2]


class Flow:
    def __init__(self, steps):
        self.steps = steps
        self.sent = next(steps)
        self.total = None

    def take(self, sent):
        if self.total is None:
            try:
                self.sent = self.steps.send(list(sent))
            except StopIteration as end:
                self.total, self.sent = end.value, []


def boundary_of(values, flows):
    values, sent = tie(values, [flow.sent for flow in flows])
    for flow, block in zip(flows, sent):
        flow.take(block)
    return values


def body(
    boundary,
    norm_gains,
    biases,
    up_bias,
    offset_table,
    attention_in,
    attention_out,
    up_weight,
    down_weight,
    offset_index,
    regions,
    micro_counts,
):
    core = lax.axis_index("section")
    first = core == 0
    me = lax.axis_index("shard")
    mb_count, per_device = boundary.shape[1], boundary.shape[2]
    slots = mb_count * per_device
    share = (slots + 1) // 2

    present = (jnp.arange(per_device)[None] < micro_counts[:, None]).reshape(slots)
    rank = jnp.cumsum(present.astype(jnp.int32)) - 1
    owner = jnp.bitwise_and(rank, 1)
    place = jnp.right_shift(rank, 1)

    hit = present & (owner == core)
    hit = hit[None] & (place[None] == jnp.arange(share)[:, None])
    own_slots = jnp.sum(jnp.where(hit, jnp.arange(slots)[None], 0), 1)
    total_images = jnp.sum(present.astype(jnp.int32))
    own_count = jnp.right_shift(total_images + 1 - core, 1)
    info = jnp.concatenate([jnp.stack([own_count, core, me]), own_slots]).astype(jnp.int32)

    flat = jnp.concatenate(
        [
            norm_gains[0].reshape(-1),
            biases[0].reshape(-1),
            up_bias[0].reshape(-1),
            offset_table[0].reshape(-1),
        ]
    )
    flat = jnp.pad(flat, (0, -flat.shape[0] % 1024)).reshape(-1, 128)

    def columns(weight):
        rows, cols = weight.shape
        return weight.reshape(2, rows // 2, cols // 512, 512).transpose(0, 2, 1, 3).reshape(2, -1, 512)

    attn_own = attention_in[0].reshape(128, 3, 512).transpose(1, 0, 2).reshape(384, 512)
    attn_own, up_weight, down_weight, attention_out, flat, boundary = tie(
        attn_own, up_weight, down_weight, attention_out, flat, boundary
    )
    attn_mine = gather_direct(attn_own)
    attn_pieces = with_other(attn_mine)
    parts = jnp.concatenate(
        [
            columns(up_weight[0]),
            down_weight[0].reshape(2, 256, 512),
            attention_out[0].reshape(2, 64, 512),
        ],
        1,
    )
    keep, got = jnp.where(first, parts[0], parts[1]), swap(jnp.where(first, parts[1], parts[0]))
    mlp_own = [jnp.where(core == layer, keep, got) for layer in range(2)]
    mlp_first, _ = tie(mlp_own[0], attn_mine[1])
    mlp_mine = gather_direct(mlp_first)

    framed = boundary.reshape(slots, TOKENS, 512)
    framed = jnp.pad(framed, ((0, 0), (0, FRAME - TOKENS), (0, 0)))
    framed = [framed, swap(framed)]

    small = by_distance(jnp.stack([flat] + [across(flat, d) for d in (1, 2, 3)]), me)
    small_other = swap(small)
    small = jnp.stack([jnp.where(first, small, small_other), jnp.where(first, small_other, small)])
    small = small.reshape(2, 4, -1).astype(F32)
    rel = offset_table.shape[1]
    gains = small[:, :, 0:256].reshape(2, 4, 2, 128).transpose(0, 2, 1, 3).reshape(2, 2, 512)
    shifts = small[:, :, 256:1024].reshape(2, 4, 6, 128).transpose(0, 2, 1, 3).reshape(2, 6, 512)
    vecs = jnp.concatenate([gains, shifts], 1)
    lifts = small[:, :, 1024:1536].reshape(2, 1, 2048)
    tables = small[:, :, 1536 : 1536 + 4 * rel].reshape(2, 4, rel, 4).transpose(0, 2, 1, 3).reshape(2, rel, HEADS)

    spare = SLOT - LEN
    pairs = jnp.pad(offset_index.T, ((0, spare), (0, spare))).reshape(-1)
    onehot = (pairs[None, :] == jnp.arange(rel)[:, None]).astype(BF16)
    heads_first = tables.transpose(0, 2, 1).reshape(2 * HEADS, rel).astype(BF16)
    offsets = jnp.dot(heads_first, onehot, preferred_element_type=F32)
    offsets = offsets.reshape(2, GROUPS, QUAD, SLOT, SLOT).transpose(0, 1, 3, 2, 4)
    offsets = offsets.reshape(2, GROUPS, SLOT, WIDE)
    bias = jnp.where(jnp.arange(SLOT)[:, None] < LEN, offsets * LOG2E, -1e30)
    split = regions.reshape(2, WIN, 2, WIN).transpose(0, 2, 1, 3).reshape(WINS, LEN)
    split = jnp.pad(split, ((0, 0), (0, spare)))
    apart = jnp.where(split[:, :, None] == jnp.tile(split, (1, QUAD))[:, None, :], 0.0, -100.0 * LOG2E)
    apart = apart.astype(F32)

    cut = [jnp.asarray(window_place(shift), BF16) for shift in (0, SHIFT)]
    x, saved = framed, []
    for layer in range(2):
        vec = vecs[layer]
        qkv, p, att, *images = attn_forward(
            layer, info, attn_pieces, x, cut[layer], cut[layer].T, vec, bias[layer], apart
        )
        if layer == 0:
            (x,) = images
            att, mlp_mine, mlp_second = tie(att, mlp_mine, mlp_own[1])
            mlp_pieces = [with_other(mlp_mine)]
            mlp_mine = gather_direct(mlp_second)
        out, mid, act, slope = mlp_forward(
            info, mlp_pieces[layer], x, att, vec, lifts[layer], slots if layer else None
        )
        if layer == 0:
            out, mlp_mine = tie(out, mlp_mine)
            mlp_pieces.append(with_other(mlp_mine))
        saved.append((x, qkv, p, att, mid, act, slope))
        x = out
    output = x
    output_other = lax.ppermute(output, "section", [(0, 1)])
    small_sums = [None, None]

    def backward_mlp(layer, g):
        x, qkv, p, att, mid, act, slope = saved[layer]
        return mlp_backward(layer, info, mlp_pieces[layer], g, att, mid, act, slope, vecs[layer])

    def backward_attn(layer, g_mid, g_att):
        x, qkv, p, *_ = saved[layer]
        return attn_backward(
            layer,
            info,
            attn_pieces,
            g_mid,
            g_att,
            x,
            qkv,
            p,
            cut[layer],
            cut[layer].T,
            vecs[layer],
            None if layer else slots,
        )

    def small_of(vec, up, table):
        table = table.reshape(HEADS, SLOT * SLOT)
        table = lax.dot_general(
            table, onehot.astype(F32), (((1,), (1,)), ((), ())), precision=lax.Precision.HIGHEST
        )
        return jnp.concatenate([vec.reshape(-1), up.reshape(-1), table.reshape(-1)])

    g_mid, g_att, *sums, mlp_vec, up_sums = backward_mlp(1, framed)
    second_mlp = Flow(reduce_steps(*sums, (2, 1)))
    g_mid, g_att = boundary_of((g_mid, g_att), [second_mlp])
    g, *sums, attn_vec, table = backward_attn(1, g_mid, g_att)
    second_small = (mlp_vec + attn_vec, up_sums, table)
    g, sums = boundary_of((g, sums), [second_mlp])
    second_attn = Flow(reduce_steps(*sums, (1, 2)))
    g = boundary_of(g, [second_attn])
    g_mid, g_att, *sums, mlp_vec, up_sums = backward_mlp(0, g)
    second_small = small_of(*second_small)
    g_mid, g_att, sums, second_small = boundary_of(
        (g_mid, g_att, sums, second_small), [second_mlp, second_attn]
    )
    first_mlp = Flow(reduce_steps(*sums, (2, 1)))
    g_mid, g_att = boundary_of((g_mid, g_att), [first_mlp])
    g, *sums, attn_vec, table = backward_attn(0, g_mid, g_att)
    g, sums = boundary_of((g, sums), [second_mlp, second_attn, first_mlp])
    first_attn = Flow(reduce_steps(*sums, (1, 2)))
    g, mlp_vec, up_sums, attn_vec, table = boundary_of(
        (g, mlp_vec, up_sums, attn_vec, table), [first_attn]
    )
    small = jnp.stack([small_of(mlp_vec + attn_vec, up_sums, table), second_small])
    width = small.shape[1]
    small = jnp.pad(small, ((0, 0), (0, -width % 1024))).reshape(-1, 128)
    g, small = boundary_of((g, small), [first_attn, first_mlp, second_attn])
    back = lax.ppermute(g, "section", [(1, 0)])
    small_flow = Flow(sum_steps(small))

    mine = owner == core
    pair = (jnp.where(first, g, output), jnp.where(first, back, output_other))
    chosen = jnp.where(mine[:, None, None], *pair)
    chosen = jnp.where(present[:, None, None], chosen, jnp.zeros((), BF16))[:, :TOKENS]
    results = chosen.reshape(1, mb_count, per_device, SIDE, SIDE, 512)
    boundary_of((), [first_attn, small_flow])
    results = boundary_of(results, [small_flow])
    boundary_of((), [first_attn, first_mlp, small_flow])
    flows = [first_attn, small_flow, first_mlp, second_attn, second_mlp]
    while any(flow.total is None for flow in flows):
        boundary_of((), flows)

    def exchanged(one, two):
        hold = jnp.where(first, one, two)
        back = swap(jnp.where(first, two, one))
        return jnp.stack([jnp.where(first, hold, back), jnp.where(first, back, hold)])

    one, two = [
        jnp.concatenate([attn.total, mlp.total], 0)
        for attn, mlp in ((first_attn, first_mlp), (second_attn, second_mlp))
    ]
    both = exchanged(one, two).astype(F32)
    grad_in = both[:, 0:192].reshape(2, 3, 64, 512).transpose(0, 2, 1, 3).reshape(128, 1536)
    grad_up = both[:, 192:448].reshape(2, 4, 64, 512).transpose(0, 2, 1, 3).reshape(128, 2048)
    grad_down = both[:, 448:704].reshape(512, 512)
    grad_out = both[:, 704:768].reshape(128, 512)

    bundle = small_flow.total.reshape(2, -1)[:, :width]
    bundle = lax.dynamic_index_in_dim(bundle, core, 0, keepdims=False)
    vec = lax.dynamic_slice_in_dim(bundle[:4096].reshape(8, 512), me * 128, 128, 1)
    grad_lift = lax.dynamic_slice_in_dim(bundle[4096:6144], me * 512, 512, 0)
    grad_table = lax.dynamic_slice_in_dim(bundle[6144:].reshape(HEADS, rel), me * 4, 4, 0).T

    return (
        results,
        vec[None, 0:2],
        vec[None, 2:8],
        grad_lift[None],
        grad_table[None],
        grad_in[None],
        grad_out[None],
        grad_up[None],
        grad_down[None],
    )


def solution(mesh):
    placed = (
        P("section", None, ("shard", "replica"), None, None, None),
        P("section", None, "shard"),
        P("section", None, "shard"),
        P("section", "shard"),
        P("section", None, "shard"),
        P("section", "shard", None),
        P("section", "shard", None),
        P("section", "shard", None),
        P("section", "shard", None),
        P(),
        P(),
        P(),
    )
    return jax.shard_map(
        body,
        mesh=mesh,
        in_specs=placed,
        out_specs=(placed[0],) + placed[1:9],
        check_vma=False,
    )
```

```python
import functools

import jax
import jax.numpy as jnp
import numpy as np
from jax import lax
from jax.experimental import pallas as pl
from jax.experimental.layout import Layout, with_layout_constraint
from jax.experimental.pallas import tpu as pltpu
from jax.sharding import PartitionSpec as P

WIN = 7
SIDE = 14
SHIFT = 3
LEN = WIN * WIN
WINS = 4
SLOT = 64
ROWS = WINS * SLOT
TOKENS = SIDE * SIDE
FRAME = 208
HEADS = 16
QUAD = 4
GROUPS = HEADS // QUAD
WIDE = QUAD * SLOT
LOG2E = 1.4426950408889634
F32 = jnp.float32
BF16 = jnp.bfloat16


def window_place(shift):
    place = np.zeros((ROWS, FRAME), np.float32)
    for window in range(WINS):
        for token in range(LEN):
            line = ((window // 2) * WIN + token // WIN + shift) % SIDE
            column = ((window % 2) * WIN + token % WIN + shift) % SIDE
            place[window * SLOT + token, line * SIDE + column] = 1.0
    return place


def mm(a, b):
    return jnp.dot(a, b, preferred_element_type=F32)


def mm_nt(a, b):
    return lax.dot_general(a, b, (((1,), (1,)), ((), ())), preferred_element_type=F32)


def mm_tn(a, b):
    return lax.dot_general(a, b, (((0,), (0,)), ((), ())), preferred_element_type=F32)


def standard(v):
    centered = v - jnp.mean(v, -1, keepdims=True)
    spread = jnp.mean(centered * centered, -1, keepdims=True)
    inverse = lax.rsqrt(spread + 1e-05)
    return centered * inverse, inverse


def gelu_pair(h):
    density = jnp.exp(-0.5 * h * h)
    t = 1.0 / (1.0 + (0.3275911 * 0.7071067811865476) * jnp.abs(h))
    poly = t * (
        0.5 * 0.254829592
        + t
        * (
            0.5 * -0.284496736
            + t * (0.5 * 1.421413741 + t * (0.5 * -1.453152027 + t * (0.5 * 1.061405429)))
        )
    )
    tail = poly * density
    cdf = jnp.where(h < 0, tail, 1.0 - tail)
    return h * cdf, cdf + h * (density * 0.3989422804014327)


def head_mask(shape):
    rows = lax.broadcasted_iota(jnp.int32, shape, 0) // SLOT
    lanes = lax.broadcasted_iota(jnp.int32, shape, 1) // 32
    return rows == lanes


def spread_heads(block, mask):
    return jnp.where(mask, jnp.concatenate([block] * QUAD, 0), jnp.zeros((), block.dtype))


def join_heads(blocks):
    lane = lax.broadcasted_iota(jnp.int32, (SLOT, 128), 1) // 32
    out = blocks[:SLOT]
    for h in range(1, QUAD):
        out = jnp.where(lane == h, blocks[h * SLOT : (h + 1) * SLOT], out)
    return out


def attn_load(layer, info, pieces, w_in, sems):
    mine, other = pieces[:4], pieces[4:]

    def copies(source):
        pairs = []
        for at in range(4):
            row = pl.multiple_of(jnp.bitwise_xor(info[2], at) * 128, 128)
            for c in range(3):
                src = source[at].at[128 * c : 128 * c + 128]
                pairs.append((src, w_in.at[pl.ds(row, 128), 512 * c : 512 * c + 512]))
        return [pltpu.make_async_copy(*pair, sems.at[n]) for n, pair in enumerate(pairs)]

    @pl.when(pl.program_id(0) == 0)
    def _():
        @pl.when(info[1] == layer)
        def _():
            for c in copies(mine):
                c.start()

        @pl.when(info[1] != layer)
        def _():
            for c in copies(other):
                c.start()

    return lambda: wait_first(copies(mine))


def mlp_copies(info, pieces, places, sems):
    w_out, w_up, w_down = places
    copies = []
    for half_at in range(2):
        half = jnp.bitwise_xor(info[1], half_at)
        for shard_at in range(4):
            shard = jnp.bitwise_xor(info[2], shard_at)
            piece = pieces[4 * half_at + shard_at]
            row = pl.multiple_of(shard * 128 + half * 64, 64)
            deep = pl.multiple_of(shard * 512 + half * 256, 256)
            pairs = [
                (piece.at[64 * c : 64 * c + 64], w_up.at[pl.ds(row, 64), 512 * c : 512 * c + 512])
                for c in range(4)
            ]
            pairs.append((piece.at[256:512], w_down.at[pl.ds(deep, 256), :]))
            pairs.append((piece.at[512:576], w_out.at[pl.ds(row, 64), :]))
            for src, dst in pairs:
                copies.append(pltpu.make_async_copy(src, dst, sems.at[len(copies)]))
    return copies


def group_lanes(g):
    return lambda part: slice(512 * part + 128 * g, 512 * part + 128 * g + 128)


BLOCKS = [
    (w, slice(w * SLOT, w * SLOT + SLOT), g, group_lanes(g))
    for w in range(WINS)
    for g in range(GROUPS)
]


def start_first(copies):
    @pl.when(pl.program_id(0) == 0)
    def _():
        for c in copies:
            c.start()


def wait_first(copies):
    @pl.when(pl.program_id(0) == 0)
    def _():
        for c in copies:
            c.wait()


def clear_first(*totals):
    @pl.when(pl.program_id(0) == 0)
    def _():
        for total in totals:
            total[...] = jnp.zeros(total.shape, F32)


def accumulate(total, at, value):
    total[at] = jnp.where(pl.program_id(0) == 0, 0.0, total[at]) + value


def pick(info, section, refs):
    if len(refs) == 1:
        return refs[0][0]
    own, other = refs
    return jnp.where(info[1] == section, own[0], other[0])


def attn_forward_kernel(layer, info, *refs):
    pieces, refs = refs[:8], refs[8:]
    count = 1 if layer else 2
    x_refs, refs = refs[:count], refs[count:]
    cut_ref, join_ref, vec_ref, bias_ref, apart_ref, *refs = refs
    qkv_ref, p_ref, att_ref, *x_out, w_in, sems, att = refs
    arrived = attn_load(layer, info, pieces, w_in, sems)

    @pl.when(pl.program_id(0) < info[0])
    def _():
        x = pick(info, 0, x_refs)
        for ref in x_out:
            ref[0] = x
        xhat, _ = standard(x.astype(F32))
        normed = (xhat * vec_ref[0:1] + vec_ref[2:3]).astype(BF16)
        normed = mm(cut_ref[...], normed).astype(BF16)
        arrived()
        for part in range(3):
            block = mm(normed, w_in[:, 512 * part : 512 * part + 512])
            if part != 1:
                row = 3 if part == 0 else 4
                block = block + vec_ref[row : row + 1]
            qkv_ref[0, :, 512 * part : 512 * part + 512] = block.astype(BF16)
        mask = head_mask((WIDE, 128))
        factor = 32**-0.5 * LOG2E

        scores, probs, outs = [], [], []
        for w, rows, g, lanes in BLOCKS:
            q = qkv_ref[0, rows, lanes(0)]
            bias = bias_ref[g] + apart_ref[w] if layer else bias_ref[g]
            scores.append(mm_nt(qkv_ref[0, rows, lanes(1)], spread_heads(q, mask)) * factor + bias)
        for s in scores:
            e = jnp.exp2(s - jnp.max(s, 0, keepdims=True))
            probs.append((e * (1.0 / jnp.sum(e, 0, keepdims=True))).astype(BF16))
        for p, (w, rows, g, lanes) in zip(probs, BLOCKS):
            outs.append(mm_tn(p, qkv_ref[0, rows, lanes(2)]))
        for p, out, (w, rows, g, lanes) in zip(probs, outs, BLOCKS):
            p_ref[0, w, g] = p
            att[rows, lanes(0)] = join_heads(out).astype(BF16)
        att_ref[0] = mm(join_ref[...], att[...]).astype(BF16)


def mlp_forward_kernel(info, *refs):
    pieces, refs = refs[:8], refs[8:]
    x_ref, att_ref, vec_ref, up_bias_ref, *refs = refs
    out_ref, mid_ref, act_ref, slope_ref, w_out, w_up, w_down, sems = refs
    copies = mlp_copies(info, pieces, (w_out, w_up, w_down), sems)
    start_first(copies)

    @pl.when(pl.program_id(0) < info[0])
    def _():
        wait_first(copies)
        mid = x_ref[0].astype(F32) + (mm(att_ref[0], w_out[...]) + vec_ref[5:6])
        mid_ref[0] = mid
        xhat, _ = standard(mid)
        normed_two = (xhat * vec_ref[1:2] + vec_ref[6:7]).astype(BF16)
        cols = [slice(512 * c, 512 * c + 512) for c in range(4)]

        def lift(c):
            return mm(normed_two, w_up[:, cols[c]]) + up_bias_ref[:, cols[c]]

        hidden, active, down = lift(0), None, 0.0
        for c in range(4):
            after = lift(c + 1) if c < 3 else None
            before, (active, slope) = active, gelu_pair(hidden)
            active = active.astype(BF16)
            act_ref[0, :, cols[c]] = active
            slope_ref[0, :, cols[c]] = slope.astype(BF16)
            if c:
                down = down + mm(before, w_down[cols[c - 1], :])
            hidden = after
        down = down + mm(active, w_down[cols[3], :])
        out_ref[0] = (mid + (down + vec_ref[7:8])).astype(BF16)


def add_row(total, at, value):
    total[at : at + 1] += jnp.sum(value, 0, keepdims=True)


def norm_back(total, rows, g_normed, xhat, inverse, gain):
    add_row(total, rows[0], g_normed * xhat)
    add_row(total, rows[1], g_normed)
    u = g_normed * gain
    lean = jnp.mean(u * xhat, -1, keepdims=True)
    return (u - jnp.mean(u, -1, keepdims=True) - xhat * lean) * inverse


def mlp_backward_kernel(layer, info, *refs):
    pieces, refs = refs[:8], refs[8:]
    count = 2 if layer else 1
    g_refs, refs = refs[:count], refs[count:]
    att_ref, mid_ref, act_ref, slope_ref, vec_ref, *refs = refs
    g_mid_ref, g_att_ref, keep_ref, give_ref, vec_out, up_out, *refs = refs
    w_out, w_up, w_down, sems, d_out, d_up, d_down = refs
    copies = mlp_copies(info, pieces, (w_out, w_up, w_down), sems)
    start_first(copies)
    clear_first(vec_out, up_out)

    @pl.when(pl.program_id(0) < info[0])
    def _():
        g = pick(info, 1, g_refs)
        cols = [slice(512 * c, 512 * c + 512) for c in range(4)]
        for c in cols:
            accumulate(d_down, (slice(None), c), mm_tn(g, act_ref[0, :, c]))
        add_row(vec_out, 7, g.astype(F32))
        xhat, inverse = standard(mid_ref[0])
        normed_two = (xhat * vec_ref[1:2] + vec_ref[6:7]).astype(BF16)
        wait_first(copies)
        g_hidden = []
        for c in cols:
            part = (mm_nt(g, w_down[c, :]) * slope_ref[0, :, c].astype(F32)).astype(BF16)
            up_out[:, c] += jnp.sum(part.astype(F32), 0, keepdims=True)
            g_hidden.append(part)
        g_normed = sum(mm_nt(part, w_up[:, c]) for part, c in zip(g_hidden, cols))
        for part, c in zip(g_hidden, cols):
            accumulate(d_up, (slice(None), c), mm_tn(normed_two, part))
        g_mid = g.astype(F32) + norm_back(vec_out, (1, 6), g_normed, xhat, inverse, vec_ref[1:2])
        g_mid_ref[0] = g_mid
        g_update = g_mid.astype(BF16)
        add_row(vec_out, 5, g_update.astype(F32))
        accumulate(d_out, Ellipsis, mm_tn(att_ref[0], g_update))
        g_att_ref[0] = mm_nt(g_update, w_out[...]).astype(BF16)

    @pl.when(pl.program_id(0) == pl.num_programs(0) - 1)
    def _():
        for out_ref, half in ((keep_ref, info[1]), (give_ref, 1 - info[1])):
            for shard in range(4):
                at = jnp.bitwise_xor(info[2], shard)
                rows = pl.ds(pl.multiple_of(128 * shard + 64 * half, 64), 64)
                for c in range(4):
                    out_ref[at, 64 * c : 64 * c + 64, :] = d_up[
                        rows, 512 * c : 512 * c + 512
                    ].astype(BF16)
                deep = pl.ds(pl.multiple_of(512 * shard + 256 * half, 256), 256)
                out_ref[at, 256:512, :] = d_down[:, deep].T.astype(BF16)
                out_ref[at, 512:576, :] = d_out[rows, :].astype(BF16)


def attn_backward_kernel(layer, info, *refs):
    pieces, refs = refs[:8], refs[8:]
    g_mid_ref, g_att_ref, x_ref, qkv_ref, p_ref, cut_ref, join_ref, vec_ref, *refs = refs
    gx_ref, keep_ref, give_ref, vec_out, table_out, *refs = refs
    w_in, sems, d_in, g_att, gqkv, table_sum = refs
    arrived = attn_load(layer, info, pieces, w_in, sems)
    clear_first(vec_out, table_sum)

    @pl.when(pl.program_id(0) < info[0])
    def _():
        g_att[...] = mm(cut_ref[...], g_att_ref[0]).astype(BF16)
        mask = head_mask((WIDE, 128))

        at = range(len(BLOCKS))
        q, k, v = [[qkv_ref[0, rows, lanes(n)] for _, rows, _, lanes in BLOCKS] for n in range(3)]
        p = [p_ref[0, w, h] for w, _, h, _ in BLOCKS]
        g_out = [spread_heads(g_att[rows, lanes(0)], mask) for _, rows, _, lanes in BLOCKS]
        g_p = [mm_nt(v[n], g_out[n]) for n in at]
        g_v = [mm(p[n], g_out[n]) for n in at]
        g_s = []
        for n in at:
            soft = p[n].astype(F32)
            part = soft * g_p[n]
            g_s.append((part - soft * jnp.sum(part, 0, keepdims=True)).astype(BF16))
        g_k = [mm(g_s[n], spread_heads(q[n], mask)) for n in at]
        g_q = [mm_tn(g_s[n], k[n]) for n in at]
        for n, (_, rows, _, lanes) in enumerate(BLOCKS):
            gqkv[rows, lanes(0)] = (join_heads(g_q[n]) * 32**-0.5).astype(BF16)
            gqkv[rows, lanes(1)] = (g_k[n] * 32**-0.5).astype(BF16)
            gqkv[rows, lanes(2)] = g_v[n].astype(BF16)
        for h in range(GROUPS):
            table_sum[h] += sum(g_s[n].astype(F32) for n in at if BLOCKS[n][2] == h)
        arrived()
        xhat, inverse = standard(x_ref[0].astype(F32))
        normed = (xhat * vec_ref[0:1] + vec_ref[2:3]).astype(BF16)
        g_normed = None
        for part in range(3):
            cols = slice(512 * part, 512 * part + 512)
            block = mm(join_ref[...], gqkv[:, cols]).astype(BF16)
            accumulate(d_in, (slice(None), cols), mm_tn(normed, block))
            if part != 1:
                add_row(vec_out, 3 if part == 0 else 4, block.astype(F32))
            term = mm_nt(block, w_in[:, cols])
            g_normed = term if g_normed is None else g_normed + term
        back = norm_back(vec_out, (0, 2), g_normed, xhat, inverse, vec_ref[0:1])
        gx_ref[0] = (g_mid_ref[0] + back).astype(BF16)

    @pl.when(pl.program_id(0) == pl.num_programs(0) - 1)
    def _():
        for h in range(HEADS):
            lanes = slice(h % QUAD * SLOT, h % QUAD * SLOT + SLOT)
            table_out[h] = table_sum[h // QUAD, :, lanes]
        for out_ref, half in ((keep_ref, info[1]), (give_ref, 1 - info[1])):
            for shard in range(4):
                at = jnp.bitwise_xor(info[2], shard)
                rows = pl.ds(pl.multiple_of(128 * shard + 64 * half, 64), 64)
                for c in range(3):
                    out_ref[at, 64 * c : 64 * c + 64, :] = d_in[
                        rows, 512 * c : 512 * c + 512
                    ].astype(BF16)


def whole(shape):
    return pl.BlockSpec(shape, lambda i, info: (0,) * len(shape))


def each(shape):
    return pl.BlockSpec(
        (1,) + shape,
        lambda i, info: (jnp.maximum(jnp.minimum(i, info[0] - 1), 0),) + (0,) * len(shape),
    )


X = ((FRAME, 512), BF16)
QKV = ((ROWS, 1536), BF16)
PROB = ((WINS, GROUPS, SLOT, WIDE), BF16)
MID = ((FRAME, 512), F32)
WIDE_X = ((FRAME, 2048), BF16)
VEC = ((8, 512), F32)
ATTN_WEIGHTS = [pltpu.VMEM((512, 1536), BF16), pltpu.SemaphoreType.DMA((12,))]
MLP_WEIGHTS = [
    pltpu.VMEM((512, 512), BF16),
    pltpu.VMEM((512, 2048), BF16),
    pltpu.VMEM((2048, 512), BF16),
    pltpu.SemaphoreType.DMA((48,)),
]


def by_slot(shape):
    def place(i, info):
        return (info[3 + jnp.maximum(jnp.minimum(i, info[0] - 1), 0)],) + (0,) * len(shape)

    return pl.BlockSpec((1,) + shape, place)


def run(kernel, info, pieces, slotted, by_image, shared, outs, shared_outs, scratch, micros, slot_outs=()):
    count = info.shape[0] - 3
    return pl.pallas_call(
        kernel,
        grid_spec=pltpu.PrefetchScalarGridSpec(
            num_scalar_prefetch=1,
            grid=(count,),
            in_specs=[pl.BlockSpec(memory_space=pl.ANY)] * len(pieces)
            + [by_slot(a.shape[1:]) for a in slotted]
            + [each(a.shape[1:]) for a in by_image]
            + [whole(a.shape) for a in shared],
            out_specs=[by_slot(shape[1:]) for shape, _ in slot_outs]
            + [each(shape) for shape, _ in outs]
            + [whole(shape) for shape, _ in shared_outs],
            scratch_shapes=scratch,
        ),
        out_shape=[jax.ShapeDtypeStruct(shape, kind) for shape, kind in slot_outs]
        + [jax.ShapeDtypeStruct((count,) + shape, kind) for shape, kind in outs]
        + [jax.ShapeDtypeStruct(shape, kind) for shape, kind in shared_outs],
        compiler_params=pltpu.CompilerParams(vmem_limit_bytes=56 * 1024 * 1024),
        cost_estimate=pl.CostEstimate(
            flops=int(micros * 1e9), bytes_accessed=int(micros * 1e6), transcendentals=0
        ),
    )(info, *pieces, *slotted, *by_image, *shared)


def attn_forward(layer, info, pieces, x, cut, join, vec, bias, apart):
    return run(
        functools.partial(attn_forward_kernel, layer),
        info,
        pieces,
        [] if layer else x,
        [x] if layer else [],
        [cut, join, vec, bias, apart],
        [QKV, PROB, X] + ([] if layer else [X]),
        [],
        ATTN_WEIGHTS + [pltpu.VMEM((ROWS, 512), BF16)],
        20,
    )


def mlp_forward(info, pieces, x, att, vec, up_bias, slots=None):
    return run(
        mlp_forward_kernel,
        info,
        pieces,
        [],
        [x, att],
        [vec, up_bias],
        ([] if slots else [X]) + [MID, WIDE_X, WIDE_X],
        [],
        MLP_WEIGHTS,
        20,
        [((slots,) + X[0], BF16)] if slots else [],
    )


def mlp_backward(layer, info, pieces, g, att, mid, act, slope, vec):
    return run(
        functools.partial(mlp_backward_kernel, layer),
        info,
        pieces,
        g if layer else [],
        ([] if layer else [g]) + [att, mid, act, slope],
        [vec],
        [MID, X],
        [((4, 576, 512), BF16)] * 2 + [VEC, ((1, 2048), F32)],
        MLP_WEIGHTS
        + [pltpu.VMEM((512, 512), F32), pltpu.VMEM((512, 2048), F32), pltpu.VMEM((512, 2048), F32)],
        30,
    )


def attn_backward(layer, info, pieces, g_mid, g_att, x, qkv, p, cut, join, vec, slots=None):
    return run(
        functools.partial(attn_backward_kernel, layer),
        info,
        pieces,
        [],
        [g_mid, g_att, x, qkv, p],
        [cut, join, vec],
        [] if slots else [X],
        [((4, 192, 512), BF16)] * 2 + [VEC, ((HEADS, SLOT, SLOT), F32)],
        ATTN_WEIGHTS
        + [
            pltpu.VMEM((512, 1536), F32),
            pltpu.VMEM((ROWS, 512), BF16),
            pltpu.VMEM((ROWS, 1536), BF16),
            pltpu.VMEM((GROUPS, SLOT, WIDE), F32),
        ],
        30,
        [((slots,) + X[0], BF16)] if slots else [],
    )


def swap(block):
    return lax.ppermute(block, "section", [(0, 1), (1, 0)])


def across(block, distance):
    return lax.ppermute(block, "shard", [(i, i ^ distance) for i in range(4)])


def along(block, distance):
    size = lax.axis_size("replica")
    return lax.ppermute(block, "replica", [(i, i ^ distance) for i in range(size)])


def tie(*values):
    return lax.optimization_barrier(values)


def by_distance(stack, at):
    for bit in (1, 2):
        other = jnp.stack([stack[d ^ bit] for d in range(4)])
        stack = jnp.where(at & bit != 0, other, stack)
    return stack


def gather_direct(own):
    return [own] + [across(own, d) for d in (1, 2, 3)]


def with_other(pieces):
    return pieces + [swap(piece) for piece in pieces]


def add_low(*terms):
    total = terms[0].astype(F32)
    for term in terms[1:]:
        total = total + term.astype(F32)
    return total.astype(BF16)


def reduce_steps(keep, give, quick):
    (got,) = yield [swap(give)]
    total = [add_low(keep[d], got[d]) for d in range(4)]
    got = yield [across(total[d], d) for d in (1, 2, 3)]
    owned = add_low(total[0], *got)
    size = lax.axis_size("replica")
    if size != 4:
        return lax.psum(owned, "replica")
    if quick:
        for d in quick:
            (got,) = yield [along(owned, d)]
            owned = add_low(owned, got)
        return owned
    at = lax.axis_index("replica")
    quarters = owned.reshape(4, -1, 512)

    def pick(d):
        return lax.dynamic_index_in_dim(quarters, at ^ d, 0, keepdims=False)

    got = yield [along(pick(d), d) for d in (1, 2, 3)]
    total = add_low(pick(0), *got)
    got = yield [along(total, d) for d in (1, 2, 3)]
    held = jnp.stack([total] + list(got))
    return by_distance(held, at).reshape(owned.shape)


def sum_steps(block):
    (got,) = yield [swap(block)]
    block = block + got
    got = yield [across(block, d) for d in (1, 2, 3)]
    block = block + got[0] + got[1] + got[2]
    if lax.axis_size("replica") != 4:
        return lax.psum(block, "replica")
    got = yield [along(block, d) for d in (1, 2, 3)]
    return block + got[0] + got[1] + got[2]


class Flow:
    def __init__(self, steps):
        self.steps = steps
        self.sent = next(steps)
        self.total = None

    def take(self, sent):
        if self.total is None:
            try:
                self.sent = self.steps.send(list(sent))
            except StopIteration as end:
                self.total, self.sent = end.value, []


def boundary_of(values, flows):
    values, sent = tie(values, [flow.sent for flow in flows])
    for flow, block in zip(flows, sent):
        flow.take(block)
    return values


def body(
    boundary,
    norm_gains,
    biases,
    up_bias,
    offset_table,
    attention_in,
    attention_out,
    up_weight,
    down_weight,
    offset_index,
    regions,
    micro_counts,
):
    core = lax.axis_index("section")
    first = core == 0
    me = lax.axis_index("shard")
    mb_count, per_device = boundary.shape[1], boundary.shape[2]
    slots = mb_count * per_device
    share = (slots + 1) // 2

    present = (jnp.arange(per_device)[None] < micro_counts[:, None]).reshape(slots)
    rank = jnp.cumsum(present.astype(jnp.int32)) - 1
    owner = jnp.bitwise_and(rank, 1)
    place = jnp.right_shift(rank, 1)

    hit = present & (owner == core)
    hit = hit[None] & (place[None] == jnp.arange(share)[:, None])
    own_slots = jnp.sum(jnp.where(hit, jnp.arange(slots)[None], 0), 1)
    total_images = jnp.sum(present.astype(jnp.int32))
    own_count = jnp.right_shift(total_images + 1 - core, 1)
    info = jnp.concatenate([jnp.stack([own_count, core, me]), own_slots]).astype(jnp.int32)

    flat = jnp.concatenate(
        [
            norm_gains[0].reshape(-1),
            biases[0].reshape(-1),
            up_bias[0].reshape(-1),
            offset_table[0].reshape(-1),
        ]
    )
    flat = jnp.pad(flat, (0, -flat.shape[0] % 1024)).reshape(-1, 128)

    def columns(weight):
        rows, cols = weight.shape
        return weight.reshape(2, rows // 2, cols // 512, 512).transpose(0, 2, 1, 3).reshape(2, -1, 512)

    attn_own = attention_in[0].reshape(128, 3, 512).transpose(1, 0, 2).reshape(384, 512)
    attn_own, up_weight, down_weight, attention_out, flat, boundary = tie(
        attn_own, up_weight, down_weight, attention_out, flat, boundary
    )
    attn_mine = gather_direct(attn_own)
    attn_pieces = with_other(attn_mine)
    parts = jnp.concatenate(
        [
            columns(up_weight[0]),
            down_weight[0].reshape(2, 256, 512),
            attention_out[0].reshape(2, 64, 512),
        ],
        1,
    )
    keep, got = jnp.where(first, parts[0], parts[1]), swap(jnp.where(first, parts[1], parts[0]))
    mlp_own = [jnp.where(core == layer, keep, got) for layer in range(2)]
    mlp_first, _ = tie(mlp_own[0], attn_mine[1])
    mlp_mine = gather_direct(mlp_first)

    framed = boundary.reshape(slots, TOKENS, 512)
    framed = jnp.pad(framed, ((0, 0), (0, FRAME - TOKENS), (0, 0)))
    framed = [framed, swap(framed)]

    small = by_distance(jnp.stack([flat] + [across(flat, d) for d in (1, 2, 3)]), me)
    small_other = swap(small)
    small = jnp.stack([jnp.where(first, small, small_other), jnp.where(first, small_other, small)])
    small = small.reshape(2, 4, -1).astype(F32)
    rel = offset_table.shape[1]
    gains = small[:, :, 0:256].reshape(2, 4, 2, 128).transpose(0, 2, 1, 3).reshape(2, 2, 512)
    shifts = small[:, :, 256:1024].reshape(2, 4, 6, 128).transpose(0, 2, 1, 3).reshape(2, 6, 512)
    vecs = jnp.concatenate([gains, shifts], 1)
    lifts = small[:, :, 1024:1536].reshape(2, 1, 2048)
    tables = small[:, :, 1536 : 1536 + 4 * rel].reshape(2, 4, rel, 4).transpose(0, 2, 1, 3).reshape(2, rel, HEADS)

    spare = SLOT - LEN
    pairs = jnp.pad(offset_index.T, ((0, spare), (0, spare))).reshape(-1)
    onehot = (pairs[None, :] == jnp.arange(rel)[:, None]).astype(BF16)
    heads_first = tables.transpose(0, 2, 1).reshape(2 * HEADS, rel).astype(BF16)
    offsets = jnp.dot(heads_first, onehot, preferred_element_type=F32)
    offsets = offsets.reshape(2, GROUPS, QUAD, SLOT, SLOT).transpose(0, 1, 3, 2, 4)
    offsets = offsets.reshape(2, GROUPS, SLOT, WIDE)
    bias = jnp.where(jnp.arange(SLOT)[:, None] < LEN, offsets * LOG2E, -1e30)
    split = regions.reshape(2, WIN, 2, WIN).transpose(0, 2, 1, 3).reshape(WINS, LEN)
    split = jnp.pad(split, ((0, 0), (0, spare)))
    apart = jnp.where(split[:, :, None] == jnp.tile(split, (1, QUAD))[:, None, :], 0.0, -100.0 * LOG2E)
    apart = apart.astype(F32)

    cut = [jnp.asarray(window_place(shift), BF16) for shift in (0, SHIFT)]
    x, saved = framed, []
    for layer in range(2):
        vec = vecs[layer]
        qkv, p, att, *images = attn_forward(
            layer, info, attn_pieces, x, cut[layer], cut[layer].T, vec, bias[layer], apart
        )
        if layer == 0:
            (x,) = images
            att, mlp_mine, mlp_second = tie(att, mlp_mine, mlp_own[1])
            mlp_pieces = [with_other(mlp_mine)]
            mlp_mine = gather_direct(mlp_second)
        out, mid, act, slope = mlp_forward(
            info, mlp_pieces[layer], x, att, vec, lifts[layer], slots if layer else None
        )
        if layer == 0:
            out, mlp_mine = tie(out, mlp_mine)
            mlp_pieces.append(with_other(mlp_mine))
        saved.append((x, qkv, p, att, mid, act, slope))
        x = out
    output = x
    output_other = lax.ppermute(output, "section", [(0, 1)])
    small_sums = [None, None]

    def backward_mlp(layer, g):
        x, qkv, p, att, mid, act, slope = saved[layer]
        return mlp_backward(layer, info, mlp_pieces[layer], g, att, mid, act, slope, vecs[layer])

    def backward_attn(layer, g_mid, g_att):
        x, qkv, p, *_ = saved[layer]
        return attn_backward(
            layer,
            info,
            attn_pieces,
            g_mid,
            g_att,
            x,
            qkv,
            p,
            cut[layer],
            cut[layer].T,
            vecs[layer],
            None if layer else slots,
        )

    def small_of(vec, up, table):
        table = table.reshape(HEADS, SLOT * SLOT)
        table = lax.dot_general(
            table, onehot.astype(F32), (((1,), (1,)), ((), ())), precision=lax.Precision.HIGHEST
        )
        return jnp.concatenate([vec.reshape(-1), up.reshape(-1), table.reshape(-1)])

    g_mid, g_att, *sums, mlp_vec, up_sums = backward_mlp(1, framed)
    second_mlp = Flow(reduce_steps(*sums, (2, 1)))
    g_mid, g_att = boundary_of((g_mid, g_att), [second_mlp])
    g, *sums, attn_vec, table = backward_attn(1, g_mid, g_att)
    second_small = (mlp_vec + attn_vec, up_sums, table)
    g, sums = boundary_of((g, sums), [second_mlp])
    second_attn = Flow(reduce_steps(*sums, (1, 2)))
    g = boundary_of(g, [second_attn])
    g_mid, g_att, *sums, mlp_vec, up_sums = backward_mlp(0, g)
    second_small = small_of(*second_small)
    g_mid, g_att, sums, second_small = boundary_of(
        (g_mid, g_att, sums, second_small), [second_mlp, second_attn]
    )
    first_mlp = Flow(reduce_steps(*sums, (2, 1)))
    g_mid, g_att = boundary_of((g_mid, g_att), [first_mlp])
    g, *sums, attn_vec, table = backward_attn(0, g_mid, g_att)
    g, sums = boundary_of((g, sums), [second_mlp, second_attn, first_mlp])
    first_attn = Flow(reduce_steps(*sums, (1, 2)))
    g, mlp_vec, up_sums, attn_vec, table = boundary_of(
        (g, mlp_vec, up_sums, attn_vec, table), [first_attn]
    )
    small = jnp.stack([small_of(mlp_vec + attn_vec, up_sums, table), second_small])
    width = small.shape[1]
    small = jnp.pad(small, ((0, 0), (0, -width % 1024))).reshape(-1, 128)
    g, small = boundary_of((g, small), [first_attn, first_mlp, second_attn])
    back = lax.ppermute(g, "section", [(1, 0)])
    small_flow = Flow(sum_steps(small))

    mine = owner == core
    pair = (jnp.where(first, g, output), jnp.where(first, back, output_other))
    chosen = jnp.where(mine[:, None, None], *pair)
    chosen = jnp.where(present[:, None, None], chosen, jnp.zeros((), BF16))[:, :TOKENS]
    results = chosen.reshape(1, mb_count, per_device, SIDE, SIDE, 512)
    boundary_of((), [first_attn, small_flow])
    results = with_layout_constraint(results, Layout(major_to_minor=(0, 2, 3, 4, 1, 5)))
    results = boundary_of(results, [small_flow])
    boundary_of((), [first_attn, first_mlp, small_flow])
    flows = [first_attn, small_flow, first_mlp, second_attn, second_mlp]
    while any(flow.total is None for flow in flows):
        boundary_of((), flows)

    def exchanged(one, two):
        hold = jnp.where(first, one, two)
        back = swap(jnp.where(first, two, one))
        return jnp.stack([jnp.where(first, hold, back), jnp.where(first, back, hold)])

    one, two = [
        jnp.concatenate([attn.total, mlp.total], 0)
        for attn, mlp in ((first_attn, first_mlp), (second_attn, second_mlp))
    ]
    both = exchanged(one, two).astype(F32)
    grad_in = both[:, 0:192].reshape(2, 3, 64, 512).transpose(0, 2, 1, 3).reshape(128, 1536)
    grad_up = both[:, 192:448].reshape(2, 4, 64, 512).transpose(0, 2, 1, 3).reshape(128, 2048)
    grad_down = both[:, 448:704].reshape(512, 512)
    grad_out = both[:, 704:768].reshape(128, 512)

    bundle = small_flow.total.reshape(2, -1)[:, :width]
    bundle = lax.dynamic_index_in_dim(bundle, core, 0, keepdims=False)
    vec = lax.dynamic_slice_in_dim(bundle[:4096].reshape(8, 512), me * 128, 128, 1)
    grad_lift = lax.dynamic_slice_in_dim(bundle[4096:6144], me * 512, 512, 0)
    grad_table = lax.dynamic_slice_in_dim(bundle[6144:].reshape(HEADS, rel), me * 4, 4, 0).T

    return (
        results,
        vec[None, 0:2],
        vec[None, 2:8],
        grad_lift[None],
        grad_table[None],
        grad_in[None],
        grad_out[None],
        grad_up[None],
        grad_down[None],
    )


def solution(mesh):
    placed = (
        P("section", None, ("shard", "replica"), None, None, None),
        P("section", None, "shard"),
        P("section", None, "shard"),
        P("section", "shard"),
        P("section", None, "shard"),
        P("section", "shard", None),
        P("section", "shard", None),
        P("section", "shard", None),
        P("section", "shard", None),
        P(),
        P(),
        P(),
    )
    return jax.shard_map(
        body,
        mesh=mesh,
        in_specs=placed,
        out_specs=(placed[0],) + placed[1:9],
        check_vma=False,
    )
```
